768 devices in a mesh: dp: 32 (over y, x), row: 4 (over z_lo), col: 6 (over z_hi, core).
Axes of the slice: x: 4, y: 8, z: 12 (z_hi: 3, z_lo: 4; z = z_hi * 4 + z_lo), core: 2. Of those that a mesh axis runs over, the one named last changes fastest.
Arguments:
- tokens_in: bfloat16 [4608, 6144], P(('dp', 'col'), 'row'), may hold values from -6 to 6
- slot_values: bfloat16 [2048, 24576], P('row', 'col'), may hold values from -0.15625 to 0.15625
- slot_rows: int32 [16, 192], P('row', 'col'), may hold values from 0 to 12, as said below
- act_cotangent: bfloat16 [4608, 24576], P(('dp', 'row'), 'col'), may hold values from -6 to 6
Outputs:
- activation: bfloat16 [4608, 24576], P(('dp', 'row'), 'col')
- token_grad: bfloat16 [4608, 6144], P(('dp', 'col'), 'row')
- slot_grad: float32 [512, 4, 24576], P('dp', 'row', 'col')
The draws below stay inside these ranges and needn't reach their ends.
Inputs may be any that keep to these rules, and one draw needn't show every extreme that they name: `slot_rows`: each entry names a block row 0 to 11 of its grid row's feature range, or 12 for an empty slot; the filled slots of one block column name different block rows; the number of filled slots differs between block columns and between grid tiles, and in every tile of 4 x 24576 / 768 entries some block column has all 4 slots filled.
All inputs are finite; a program needn't handle non-finite values.
Results may differ from the reference program's by a relative error of at most 0.023.
Values may be sent and summed in bfloat16 or wider, within the bound.
A program may use at most 64 MiB of HBM per device.

```python
import jax
import jax.numpy as jnp
from jax import lax

D = 6144
FF = 24576
BLK = 128
CAP = 4
BT = 12
TOK_G = 144
TOKENS = 4608
N_DP = 32
N_ROW = 4
N_COL = 6


def draw_slot_rows(key, part):
    key = jax.random.fold_in(key, 11)
    keys = jax.random.split(key, 5)
    col_total = FF // BLK
    col_tile = col_total // N_COL
    level = jax.random.randint(keys[0], (N_ROW, N_COL), CAP // 4, CAP)
    level_cols = jnp.repeat(level, col_tile, axis=1)
    extra = jax.random.randint(keys[1], (N_ROW, col_total), 0, 3)
    filled_count = jnp.minimum(level_cols + extra, CAP)
    full_column = jnp.repeat(jax.random.randint(keys[2], (N_ROW, N_COL), 0, col_tile), col_tile, axis=1)
    position = jnp.arange(col_total, dtype=jnp.int32) % col_tile
    filled_count = jnp.where(position[None, :] == full_column, CAP, filled_count)
    row_scores = jax.random.randint(keys[3], (N_ROW, col_total, BT), 0, 1 << 20) * BT + jnp.arange(BT, dtype=jnp.int32)
    chosen = jnp.argsort(row_scores, axis=-1)[..., :CAP]
    slot_scores = jax.random.randint(keys[4], (N_ROW, col_total, CAP), 0, 1 << 20) * CAP + jnp.arange(CAP, dtype=jnp.int32)
    slot_rank = jnp.argsort(jnp.argsort(slot_scores, axis=-1), axis=-1)
    filled = slot_rank < filled_count[..., None]
    result = jnp.where(filled, chosen, BT)
    return result.transpose(0, 2, 1).reshape(N_ROW * CAP, col_total).astype(jnp.int32)


def levels(key, shape, cuts, least, largest):
    factor_of = 1.0
    for dim, parts in cuts:
        steps = jax.random.uniform(jax.random.fold_in(jax.random.fold_in(key, 6), dim), (parts,), jnp.float32, least / len(cuts), largest / len(cuts))
        factor_of = factor_of * jnp.repeat(jnp.exp(steps), shape[dim] // parts).reshape((-1,) + (1,) * (len(shape) - 1 - dim))
    return factor_of


def centred(stream_key, shape, deviation, most, pieces=(), held_as=jnp.bfloat16):
    values = deviation * jax.random.normal(stream_key, shape, jnp.float32)
    if pieces:
        values = values * levels(stream_key, shape, pieces, -0.22, 0.18)
    return jnp.clip(values, -most, most).astype(held_as)


def setup_inputs(seed: int = 0) -> dict:
    seeds = jax.random.split(jax.random.key(seed), 5)
    return {
        "tokens_in": centred(seeds[0], (TOKENS, D), 1.0, 6.0, ((0, 192), (1, 4))),
        "slot_values": centred(seeds[1], (N_ROW * CAP * BLK, FF), (D // 4) ** -0.5, 0.15625, ((0, 4), (1, 6))),
        "slot_rows": draw_slot_rows(jax.random.fold_in(seeds[4], 71), 0),
        "act_cotangent": centred(seeds[3], (TOKENS, FF), 1.0, 6.0, ((0, 128), (1, 6))),
    }


root_two_pi = 0.7978845608028654
cubic_coef = 0.044715


def gelu_pair(hidden):
    inner = root_two_pi * (hidden + cubic_coef * hidden * hidden * hidden)
    tangent = jnp.tanh(inner)
    value = 0.5 * hidden * (1.0 + tangent)
    slope = 0.5 * (1.0 + tangent) + 0.5 * hidden * (1.0 - tangent * tangent) * root_two_pi * (1.0 + 3.0 * cubic_coef * hidden * hidden)
    return value, slope


def reference(tokens_in, slot_values, slot_rows, act_cotangent):
    highest = lax.Precision.HIGHEST
    col_total = FF // BLK
    col_tile = col_total // N_COL
    selector = (slot_rows.reshape(N_ROW, CAP, col_total)[..., None] == jnp.arange(BT, dtype=jnp.int32)).astype(jnp.float32)
    weights = slot_values.astype(jnp.float32).reshape(N_ROW, CAP, BLK, col_total, BLK)
    token_groups = tokens_in.reshape(N_DP, TOK_G, D)
    cotan_groups = act_cotangent.reshape(N_DP, TOK_G, FF)

    def one_group(carry, inputs):
        group_in, group_cot = inputs
        blocks = group_in.astype(jnp.float32).reshape(TOK_G, N_ROW, BT, BLK)
        hidden = jnp.zeros((TOK_G, col_total, BLK), jnp.float32)
        picked_list = []
        for grid_row in range(N_ROW):
            picked = jnp.einsum('tbk,sjb->tjsk', blocks[:, grid_row], selector[grid_row], precision=highest)
            picked_list.append(picked)
            partial_sum = jnp.einsum('tjsk,skjn->tjn', picked, weights[grid_row], precision=highest)
            hidden = hidden + partial_sum.astype(jnp.bfloat16).astype(jnp.float32)
        value, slope = gelu_pair(hidden)
        activation = value.astype(jnp.bfloat16)
        cot = group_cot.astype(jnp.float32).reshape(TOK_G, col_total, BLK)
        hidden_grad = (cot * slope).astype(jnp.bfloat16).astype(jnp.float32)
        grad_parts = []
        term_list = []
        for grid_row in range(N_ROW):
            backward = jnp.einsum('tjn,skjn->tjsk', hidden_grad, weights[grid_row], precision=highest)
            backward = backward.reshape(TOK_G, N_COL, col_tile, CAP, BLK)
            tile_sel = selector[grid_row].reshape(CAP, N_COL, col_tile, BT)
            spread = jnp.einsum('tcjsk,scjb->tcbk', backward, tile_sel, precision=highest)
            spread = spread.astype(jnp.bfloat16).astype(jnp.float32).sum(axis=1)
            grad_parts.append(spread.reshape(TOK_G, BT * BLK))
            term = jnp.einsum('tjsk,tjn->skjn', picked_list[grid_row], hidden_grad, precision=highest)
            term_list.append(term.astype(jnp.bfloat16).astype(jnp.float32).reshape(CAP * BLK, FF))
        token_grad = jnp.concatenate(grad_parts, axis=1).astype(jnp.bfloat16)
        return carry + jnp.stack(term_list), (activation.reshape(TOK_G, FF), token_grad)

    start_sum = jnp.zeros((N_ROW, CAP * BLK, FF), jnp.float32)
    total, outputs = lax.scan(one_group, start_sum, (token_groups, cotan_groups))
    activation = outputs[0].reshape(TOKENS, FF)
    token_grad = outputs[1].reshape(TOKENS, D)
    slot_grad = (total * (TOKENS ** -0.5)).transpose(1, 0, 2)
    return activation, token_grad, slot_grad
```

```python
import jax
import jax.numpy as jnp
from jax import lax
from jax.experimental import pallas as pl
from jax.experimental.pallas import tpu as pltpu
from jax.sharding import PartitionSpec as P

MESH = pl.DeviceIdType.MESH
BF16 = jnp.bfloat16
F32 = jnp.float32

BLK = 128
CAP = 4
BT = 12
COLS = 32
X, Y = 4, 8
R = 4
Z = 3
TOK = 144
NC = 8
NJ = COLS // NC
NB = NJ // 2

root_two_pi = 0.7978845608028654
cubic_coef = 0.044715


def gelu_pair(hidden):
    inner = root_two_pi * (hidden + cubic_coef * hidden * hidden * hidden)
    tangent = jnp.tanh(inner)
    value = 0.5 * hidden * (1.0 + tangent)
    slope = 0.5 * (1.0 + tangent) + 0.5 * hidden * (1.0 - tangent * tangent) * root_two_pi * (
        1.0 + 3.0 * cubic_coef * hidden * hidden
    )
    return (value, slope)


class Ring:
    def __init__(self, total, first, later, size, here, right, left, send, recv, base):
        self.total, self.first, self.later = total, first, later
        self.size, self.here, self.right, self.left = size, here, right, left
        self.send, self.recv, self.base = send, recv, base
        self.half = size // 2

    def shard(self, k, step, way):
        offset = self.half + 1 - step
        place = lax.rem(self.here + (offset if way == 0 else self.size - offset), self.size)
        ref = self.total.at[k, place]
        if step == 1:
            part = self.total.shape[2] // 2
            return ref.at[pl.ds(way * part, part)]
        return ref

    def landing(self, k, step, way):
        return self.first.at[k, way] if step == 1 else self.later.at[k, step - 2, way]

    def copy(self, k, step, way):
        kind = self.base + 2 * (step - 1) + way
        return pltpu.make_async_remote_copy(
            src_ref=self.shard(k, step, way),
            dst_ref=self.landing(k, step, way),
            send_sem=self.send.at[kind],
            recv_sem=self.recv.at[k, kind],
            device_id=self.right if way == 0 else self.left,
            device_id_type=MESH,
        )

    def drain(self, k, step):
        for way in range(2):
            self.copy(k, step, way).wait_send()

    def advance(self, k, step):
        for way in range(2):
            if step > 1:
                self.copy(k, step - 1, way).wait_recv()
                ref = self.shard(k, step, way)
                if step == 2:
                    part = self.total.shape[2] // 2
                    ref = ref.at[pl.ds(way * part, part)]
                got = self.landing(k, step - 1, way)
                ref[...] = (ref[...].astype(F32) + got[...].astype(F32)).astype(BF16)
            self.copy(k, step, way).start()
        if step > 1:
            self.drain(k, step - 1)

    def finish(self, k):
        last = self.half
        for way in range(2):
            self.copy(k, last, way).wait_recv()
        result = self.total[k, self.here].astype(F32)
        result = result + self.landing(k, last, 0)[...].astype(F32)
        result = result + self.landing(k, last, 1)[...].astype(F32)
        self.drain(k, last)
        return result


def kernel(
    tok_in, rows, inv, cot_in, sv_hbm,
    act_out, tg_out, sg_out,
    agb, tok, tokt, sv, cot, part, rr, rl, hg,
    ta, ax1, ax2, ya, ay1, ay2, tb, by1, by2, xb, bx1, bx2,
    tgacc, tgs, tgr1, tgr2,
    sv_sem, tk_send, tk_recv, row_send, row_recv, ring_send, ring_recv, tg_send, tg_recv,
):
    dp, row, col = lax.axis_index("dp"), lax.axis_index("row"), lax.axis_index("col")
    x, y = lax.rem(dp, X), lax.div(dp, X)
    core, z = lax.rem(col, 2), lax.div(col, 2)
    x_right = (y * X + lax.rem(x + 1, X), row, col)
    x_left = (y * X + lax.rem(x + X - 1, X), row, col)
    y_right = (lax.rem(y + 1, Y) * X + x, row, col)
    y_left = (lax.rem(y + Y - 1, Y) * X + x, row, col)
    row_right, row_left = (dp, row + 1, col), (dp, row - 1, col)
    sibling = (dp, row, z * 2 + 1 - core)
    z_right, z_left = lax.rem(z + 1, Z), lax.rem(z + Z - 1, Z)
    dev_z_right, dev_z_left = (dp, row, z_right * 2 + core), (dp, row, z_left * 2 + core)

    load = pltpu.make_async_copy(sv_hbm, sv.at[pl.ds(0, CAP)], sv_sem)
    load.start()

    barrier = pltpu.get_barrier_semaphore()
    for other in (x_right, x_left, y_right, y_left, sibling, dev_z_right, dev_z_left):
        pl.semaphore_signal(barrier, inc=1, device_id=other, device_id_type=MESH)

    @pl.when(row < R - 1)
    def _():
        pl.semaphore_signal(barrier, inc=1, device_id=row_right, device_id_type=MESH)

    @pl.when(row > 0)
    def _():
        pl.semaphore_signal(barrier, inc=1, device_id=row_left, device_id_type=MESH)

    own = tok_in[...].astype(F32)
    for p in range(BT // 2):
        pair = [own[:, (2 * p + i) * BLK : (2 * p + i + 1) * BLK] for i in range(2)]
        agb[col, pl.ds(3 * p, 3)] = jnp.concatenate(pair, 0).astype(BF16).reshape(3, 16, BLK)

    pl.semaphore_wait(barrier, 7 + (row < R - 1).astype(jnp.int32) + (row > 0).astype(jnp.int32))

    def token_copy(slot, send, device):
        return pltpu.make_async_remote_copy(
            src_ref=agb.at[slot],
            dst_ref=agb.at[slot],
            send_sem=tk_send.at[send],
            recv_sem=tk_recv.at[slot],
            device_id=device,
            device_id_type=MESH,
        )

    token_copy(col, 0, dev_z_right).start()
    token_copy(col, 1, dev_z_left).start()
    token_copy(col, 2, sibling).start()

    last_rows = cot_in[pl.ds(32, 4), :].astype(F32)
    for k in range(NC):
        for jj in range(NJ):
            j = k * NJ + jj
            cot[k, pl.ds(2 * jj, 2)] = cot_in[pl.ds(0, 32), pl.ds(j * BLK, BLK)].reshape(2, 16, BLK)
        cot[k, 2 * NJ] = jnp.concatenate(
            [last_rows[:, (k * NJ + jj) * BLK : (k * NJ + jj + 1) * BLK] for jj in range(NJ)], 0
        ).astype(BF16)
    sv[CAP] = jnp.zeros((BLK, COLS * BLK), BF16)
    rr[:, 0] = jnp.zeros((NC, 2 * NJ + 1, 16, BLK), BF16)
    rl[:, R - 1] = jnp.zeros((NC, 2 * NJ + 1, 16, BLK), BF16)
    tgacc[...] = jnp.zeros(tgacc.shape, F32)
    tok[BT] = jnp.zeros((TOK, BLK), BF16)
    tokt[BT] = jnp.zeros((BLK, 2 * BLK), BF16)

    from_left, from_right = z_left * 2 + core, z_right * 2 + core
    token_copy(from_left, 0, dev_z_right).wait_recv()
    token_copy(from_left, 3, sibling).start()
    token_copy(from_right, 0, dev_z_left).wait_recv()
    token_copy(from_right, 4, sibling).start()
    for other in range(Z):
        token_copy(other * 2 + 1 - core, 2, sibling).wait_recv()
    for send in range(5):
        token_copy(col, send, sibling).wait_send()

    def unpack(p, carry):
        pieces = [agb[c, pl.ds(3 * p, 3)].astype(F32).reshape(48, BLK) for c in range(2 * Z)]
        for i in range(2):
            full = jnp.concatenate([v[24 * i : 24 * i + 24] for v in pieces], 0)
            ordered = jnp.concatenate(
                [full[36 * r : 36 * r + 32] for r in range(R)]
                + [full[36 * r + 32 : 36 * r + 36] for r in range(R)]
                + [jnp.zeros((2 * BLK - TOK, BLK), F32)],
                0,
            )
            tok[2 * p + i] = ordered[:TOK].astype(BF16)
            tokt[2 * p + i] = ordered.T.astype(BF16)
        return carry

    lax.fori_loop(0, BT // 2, unpack, 0)
    load.wait()

    ring_ax = Ring(ta, ax1, ax2, X, x, x_right, x_left, ring_send, ring_recv, 0)
    ring_ay = Ring(ya, ay1, ay2, Y, y, y_right, y_left, ring_send, ring_recv, 4)
    ring_by = Ring(tb, by1, by2, Y, y, y_right, y_left, ring_send, ring_recv, 12)
    ring_bx = Ring(xb, bx1, bx2, X, x, x_right, x_left, ring_send, ring_recv, 20)

    def columns(j):
        return pl.ds(pl.multiple_of(j * BLK, BLK), BLK)

    def row_sum_copy(k, step, way):
        if way == 0:
            dests, land, device = pl.ds(step, R - step), rr, row_right
        else:
            dests, land, device = pl.ds(0, R - step), rl, row_left
        return pltpu.make_async_remote_copy(
            src_ref=part.at[k, dests],
            dst_ref=land.at[k, dests],
            send_sem=row_send.at[way],
            recv_sem=row_recv.at[k, way],
            device_id=device,
            device_id_type=MESH,
        )

    def row_sum_drain(k, step):
        @pl.when(row == step - 1)
        def _():
            row_sum_copy(k, step, 0).wait_send()

        @pl.when(row == R - step)
        def _():
            row_sum_copy(k, step, 1).wait_send()

    def row_sum(k, step):
        @pl.when(row == step - 1)
        def _():
            if step > 1:
                row_sum_copy(k, step - 1, 0).wait_recv()
                dests = pl.ds(step, R - step)
                part[k, dests] = (part[k, dests].astype(F32) + rr[k, dests].astype(F32)).astype(BF16)
            row_sum_copy(k, step, 0).start()

        @pl.when(row == R - step)
        def _():
            if step > 1:
                row_sum_copy(k, step - 1, 1).wait_recv()
                dests = pl.ds(0, R - step)
                part[k, dests] = (part[k, dests].astype(F32) + rl[k, dests].astype(F32)).astype(BF16)
            row_sum_copy(k, step, 1).start()

        if step > 1:
            row_sum_drain(k, step - 1)

    def gather_copy(k, source, step, way):
        return pltpu.make_async_remote_copy(
            src_ref=hg.at[k, source],
            dst_ref=hg.at[k, source],
            send_sem=row_send.at[2 + 2 * step + way],
            recv_sem=row_recv.at[k, 2 + source],
            device_id=row_right if way == 0 else row_left,
            device_id_type=MESH,
        )

    def gather_sources(step):
        return (
            (0, row - step, (row >= step), row < R - 1),
            (1, row + step, (row + step < R), row > 0),
        )

    def gather_drain(k, step):
        for way, source, have, onward in gather_sources(step):

            @pl.when(have & onward)
            def _():
                gather_copy(k, source, step, way).wait_send()

    def gather(k, step):
        for way, source, have, onward in gather_sources(step):
            if step > 0:

                @pl.when(have)
                def _():
                    gather_copy(k, source, step - 1, way).wait_recv()

            if step < R - 1:

                @pl.when(have & onward)
                def _():
                    gather_copy(k, source, step, way).start()

        if step > 0:
            gather_drain(k, step - 1)

    def forward(k):
        ends = []
        for jj in range(NJ):
            j = k * NJ + jj
            picked = jnp.concatenate([tok[rows[s, j]] for s in range(CAP)], 1)
            weight = sv[pl.ds(0, CAP), :, columns(j)].reshape(CAP * BLK, BLK)
            result = jnp.dot(picked, weight, preferred_element_type=F32)
            for d in range(R):
                part[k, d, pl.ds(2 * jj, 2)] = result[32 * d : 32 * d + 32].astype(BF16).reshape(2, 16, BLK)
            ends.append(result[32 * R :])
        for d in range(R):
            part[k, d, 2 * NJ] = jnp.concatenate([e[4 * d : 4 * d + 4] for e in ends], 0).astype(BF16)
        row_sum(k, 1)

    def activate(k):
        @pl.when(row == R - 1)
        def _():
            row_sum_copy(k, R - 1, 0).wait_recv()

        @pl.when(row == 0)
        def _():
            row_sum_copy(k, R - 1, 1).wait_recv()

        hidden = part[k, row].astype(F32) + rr[k, row].astype(F32) + rl[k, row].astype(F32)
        value, slope = gelu_pair(hidden)
        hg[k, row] = (cot[k].astype(F32) * slope).astype(BF16)
        gather(k, 0)
        act_out[k] = value.astype(BF16)
        row_sum_drain(k, R - 1)

    def grad_blocks(k):
        ends = [hg[k, s, 2 * NJ].astype(F32) for s in range(R)]
        blocks = []
        for jj in range(NJ):
            mains = [hg[k, s, pl.ds(2 * jj, 2)].reshape(32, BLK) for s in range(R)]
            end = jnp.concatenate([e[4 * jj : 4 * jj + 4] for e in ends], 0).astype(BF16)
            blocks.append(jnp.concatenate(mains + [end], 0))
        return blocks

    def weight_grad(k):
        blocks = grad_blocks(k)
        for jj in range(NJ):
            j = k * NJ + jj
            picked = jnp.concatenate([tokt[rows[s, j]] for s in range(CAP)], 0)
            grad = jnp.concatenate([blocks[jj], jnp.zeros((2 * BLK - TOK, BLK), BF16)], 0)
            term = jnp.dot(picked, grad, preferred_element_type=F32).astype(BF16).reshape(Y, X, 16, BLK)
            if jj < NB:
                for xx in range(X):
                    ta[k, xx, :, jj] = term[:, xx]
            else:
                tb[k, :, :, jj - NB] = term
        ring_ax.advance(k, 1)
        ring_by.advance(k, 1)

    def token_grad(k):
        grad = jnp.concatenate(grad_blocks(k), 1)

        def pair(p, carry):
            weights = [
                jnp.concatenate(
                    [sv[inv[2 * p + i, k * NJ + jj], :, columns(k * NJ + jj)] for jj in range(NJ)],
                    1,
                )
                for i in range(2)
            ]
            tgacc[p] += lax.dot_general(
                grad, jnp.concatenate(weights, 0), (((1,), (1,)), ((), ())), preferred_element_type=F32
            )
            return carry

        lax.fori_loop(0, BT // 2, pair, 0)

    def tg_copy(step):
        if step == 0:
            src, dst, device = tgs.at[1 - core], tgr1, sibling
        elif step == 1:
            src, dst, device = tgs.at[core, z_right], tgr2.at[0], dev_z_right
        else:
            src, dst, device = tgs.at[core, z_left], tgr2.at[1], dev_z_left
        return pltpu.make_async_remote_copy(
            src_ref=src,
            dst_ref=dst,
            send_sem=tg_send.at[step],
            recv_sem=tg_recv.at[step],
            device_id=device,
            device_id_type=MESH,
        )

    def tg_first():
        def pair(p, carry):
            both = tgacc[p]
            pieces = []
            for i in range(2):
                v = both[:, i * BLK : (i + 1) * BLK]
                order = []
                for r in range(R):
                    order += [v[32 * r : 32 * r + 32], v[32 * R + 4 * r : 32 * R + 4 * r + 4]]
                pieces.append(jnp.concatenate(order, 0))
            for c in range(2 * Z):
                shard = jnp.concatenate([v[24 * c : 24 * c + 24] for v in pieces], 0)
                tgs[c % 2, c // 2, pl.ds(3 * p, 3)] = shard.astype(BF16).reshape(3, 16, BLK)
            return carry

        lax.fori_loop(0, BT // 2, pair, 0)
        tg_copy(0).start()

    def tg_second():
        tg_copy(0).wait_recv()
        tgs[core] = (tgs[core].astype(F32) + tgr1[...].astype(F32)).astype(BF16)
        tg_copy(1).start()
        tg_copy(2).start()
        tg_copy(0).wait_send()

    def tg_last():
        tg_copy(1).wait_recv()
        tg_copy(2).wait_recv()
        total = tgs[core, z].astype(F32) + tgr2[0].astype(F32) + tgr2[1].astype(F32)
        tg_out[...] = total.astype(BF16)
        tg_copy(1).wait_send()
        tg_copy(2).wait_send()

    factor = float(TOK * X * Y) ** (-0.5)

    def ring_7(k):
        ring_ax.advance(k, 2)
        ring_by.advance(k, 2)

    def ring_8(k):
        ya[k] = ring_ax.finish(k).astype(BF16)
        ring_ay.advance(k, 1)
        ring_by.advance(k, 3)

    def ring_9(k):
        ring_ay.advance(k, 2)
        ring_by.advance(k, 4)

    def ring_10(k):
        xb[k] = ring_by.finish(k).astype(BF16)
        ring_bx.advance(k, 1)
        ring_ay.advance(k, 3)

    def ring_11(k):
        ring_ay.advance(k, 4)
        ring_bx.advance(k, 2)

    def ring_12(k):
        left = ring_ay.finish(k) * factor
        right = ring_bx.finish(k) * factor
        for b in range(NB):
            sg_out[:, columns(k * NJ + b)] = left[b]
            sg_out[:, columns(k * NJ + NB + b)] = right[b]

    stages = (
        (6, lambda k: gather(k, 3)),
        (5, lambda k: gather(k, 2)),
        (4, lambda k: gather(k, 1)),
        (3, activate),
        (2, lambda k: row_sum(k, 3)),
        (1, lambda k: row_sum(k, 2)),
        (12, ring_12),
        (11, ring_11),
        (10, ring_10),
        (9, ring_9),
        (8, ring_8),
        (7, ring_7),
        (6, weight_grad),
        (0, forward),
        (6, token_grad),
    )

    def tick(t, carry):
        for stage, work in stages:
            k = t - stage

            @pl.when((k >= 0) & (k < NC))
            def _():
                work(k)

        for at, work in ((6, tg_first), (7, tg_second), (8, tg_last)):

            @pl.when(t == NC + at)
            def _():
                work()

        return carry

    lax.fori_loop(0, NC + 12, tick, 0)


def body(tokens_in, slot_values, slot_rows, act_cotangent):
    blocks = jnp.arange(BT, dtype=jnp.int32)
    slots = jnp.arange(CAP, dtype=jnp.int32)
    match = slot_rows[None, :, :] == blocks[:, None, None]
    inverse = CAP + jnp.sum(jnp.where(match, slots[None, :, None] - CAP, 0), axis=1)

    def dma(*shape):
        return pltpu.SemaphoreType.DMA(shape)

    def buf(*shape, dtype=BF16):
        return pltpu.VMEM(shape, dtype)

    vmem = pl.BlockSpec(memory_space=pltpu.VMEM)
    smem = pl.BlockSpec(memory_space=pltpu.SMEM)
    tiles = 2 * NJ + 1
    packed, grad, summed = pl.pallas_call(
        kernel,
        out_shape=(
            jax.ShapeDtypeStruct((NC, tiles, 16, BLK), BF16),
            jax.ShapeDtypeStruct((18, 16, BLK), BF16),
            jax.ShapeDtypeStruct((16, COLS * BLK), F32),
        ),
        in_specs=[vmem, smem, smem, vmem, pl.BlockSpec(memory_space=pl.ANY)],
        out_specs=(vmem, vmem, vmem),
        scratch_shapes=[
            buf(2 * Z, 18, 16, BLK),
            buf(BT + 1, TOK, BLK),
            buf(BT + 1, BLK, 2 * BLK),
            buf(CAP + 1, BLK, COLS * BLK),
            buf(NC, tiles, 16, BLK),
            buf(NC, R, tiles, 16, BLK),
            buf(NC, R, tiles, 16, BLK),
            buf(NC, R, tiles, 16, BLK),
            buf(NC, R, tiles, 16, BLK),
            buf(NC, X, Y, NB, 16, BLK),
            buf(NC, 2, Y // 2, NB, 16, BLK),
            buf(NC, 1, 2, Y, NB, 16, BLK),
            buf(NC, Y, NB, 16, BLK),
            buf(NC, 2, NB // 2, 16, BLK),
            buf(NC, 3, 2, NB, 16, BLK),
            buf(NC, Y, X, NB, 16, BLK),
            buf(NC, 2, X // 2, NB, 16, BLK),
            buf(NC, 3, 2, X, NB, 16, BLK),
            buf(NC, X, NB, 16, BLK),
            buf(NC, 2, NB // 2, 16, BLK),
            buf(NC, 1, 2, NB, 16, BLK),
            buf(BT // 2, TOK, 2 * BLK, dtype=F32),
            buf(2, Z, 18, 16, BLK),
            buf(Z, 18, 16, BLK),
            buf(2, 18, 16, BLK),
            pltpu.SemaphoreType.DMA,
            dma(5),
            dma(2 * Z),
            dma(8),
            dma(NC, 6),
            dma(24),
            dma(NC, 24),
            dma(3),
            dma(3),
        ],
        compiler_params=pltpu.CompilerParams(
            collective_id=0, has_side_effects=True, vmem_limit_bytes=52 * 1024 * 1024
        ),
    )(tokens_in, slot_rows, inverse, act_cotangent, slot_values.reshape(CAP, BLK, COLS * BLK))

    mains = packed[:, : 2 * NJ].reshape(NC, NJ, 32, BLK)
    ends = packed[:, 2 * NJ].reshape(NC, NJ, 4, BLK)
    activation = jnp.concatenate([mains, ends], axis=2).transpose(2, 0, 1, 3).reshape(36, COLS * BLK)
    token_grad = grad.reshape(BT // 2, 2, 24, BLK).transpose(2, 0, 1, 3).reshape(24, BT * BLK)
    slot_grad = summed.reshape(16, 1, COLS * BLK)
    return (activation, token_grad, slot_grad)


def solution(mesh):
    return jax.shard_map(
        body,
        mesh=mesh,
        in_specs=(
            P(("dp", "col"), "row"),
            P("row", "col"),
            P("row", "col"),
            P(("dp", "row"), "col"),
        ),
        out_specs=(P(("dp", "row"), "col"), P(("dp", "col"), "row"), P("dp", "row", "col")),
        check_vma=False,
    )
```

```python
import jax
import jax.numpy as jnp
from jax import lax
from jax.experimental import pallas as pl
from jax.experimental.pallas import tpu as pltpu
from jax.sharding import PartitionSpec as P

MESH = pl.DeviceIdType.MESH
BF16 = jnp.bfloat16
F32 = jnp.float32

BLK = 128
CAP = 4
BT = 12
COLS = 32
X, Y = 4, 8
R = 4
Z = 3
TOK = 144
NC = 8
NJ = COLS // NC
LAG = 2

root_two_pi = 0.7978845608028654
cubic_coef = 0.044715


def gelu_pair(hidden):
    inner = root_two_pi * (hidden + cubic_coef * hidden * hidden * hidden)
    tangent = jnp.tanh(inner)
    value = 0.5 * hidden * (1.0 + tangent)
    slope = 0.5 * (1.0 + tangent) + 0.5 * hidden * (1.0 - tangent * tangent) * root_two_pi * (
        1.0 + 3.0 * cubic_coef * hidden * hidden
    )
    return (value, slope)


class Ring:
    def __init__(self, total, first, later, size, here, right, left, send, recv, base):
        self.total, self.first, self.later = total, first, later
        self.size, self.here, self.right, self.left = size, here, right, left
        self.send, self.recv, self.base = send, recv, base
        self.half = size // 2

    def shard(self, k, step, way):
        offset = self.half + 1 - step
        place = lax.rem(self.here + (offset if way == 0 else self.size - offset), self.size)
        ref = self.total.at[k, place]
        if step == 1:
            part = self.total.shape[2] // 2
            return ref.at[pl.ds(way * part, part)]
        return ref

    def landing(self, k, step, way):
        return self.first.at[k, way] if step == 1 else self.later.at[k, step - 2, way]

    def copy(self, k, step, way):
        kind = self.base + 2 * (step - 1) + way
        return pltpu.make_async_remote_copy(
            src_ref=self.shard(k, step, way),
            dst_ref=self.landing(k, step, way),
            send_sem=self.send.at[lax.rem(k, 2), kind],
            recv_sem=self.recv.at[k, kind],
            device_id=self.right if way == 0 else self.left,
            device_id_type=MESH,
        )

    def drain(self, k, step):
        for way in range(2):
            self.copy(k, step, way).wait_send()

    def advance(self, k, step):
        for way in range(2):
            if step > 1:
                self.copy(k, step - 1, way).wait_recv()
                ref = self.shard(k, step, way)
                if step == 2:
                    part = self.total.shape[2] // 2
                    ref = ref.at[pl.ds(way * part, part)]
                got = self.landing(k, step - 1, way)
                ref[...] = (ref[...].astype(F32) + got[...].astype(F32)).astype(BF16)
            self.copy(k, step, way).start()
        if step > 1:
            self.drain(k, step - 1)

    def finish(self, k):
        last = self.half
        for way in range(2):
            self.copy(k, last, way).wait_recv()
        result = self.total[k, self.here].astype(F32)
        result = result + self.landing(k, last, 0)[...].astype(F32)
        result = result + self.landing(k, last, 1)[...].astype(F32)
        self.drain(k, last)
        return result


class Direct:
    def __init__(self, total, landing, size, here, device, send, recv, base):
        self.total, self.landing, self.size, self.here = total, landing, size, here
        self.device, self.send, self.recv, self.base = device, send, recv, base

    def copy(self, k, offset):
        place = lax.rem(self.here + offset, self.size)
        kind = self.base + offset - 1
        return pltpu.make_async_remote_copy(
            src_ref=self.total.at[k, place],
            dst_ref=self.landing.at[k, offset - 1],
            send_sem=self.send.at[lax.rem(k, 2), kind],
            recv_sem=self.recv.at[k, kind],
            device_id=self.device(place),
            device_id_type=MESH,
        )

    def start(self, k):
        far_first = sorted(range(1, self.size), key=lambda o: -min(o, self.size - o))
        for offset in far_first:
            self.copy(k, offset).start()

    def drain(self, k):
        for offset in range(1, self.size):
            self.copy(k, offset).wait_send()

    def finish(self, k):
        for offset in range(1, self.size):
            self.copy(k, offset).wait_recv()
        result = self.total[k, self.here].astype(F32)
        for offset in range(1, self.size):
            result = result + self.landing[k, offset - 1].astype(F32)
        return result


def kernel(
    tok_in, rows, inv, cot_in, sv_hbm,
    act_out, tg_out, sg_out,
    agb, tok, tokt, sv, cot, part, rr, rl, hg,
    ta, ax1, ax2, ya, ay, tb, by1, by2, xb, bx,
    hgt, tgacc, tgs, tgr1, tgr2,
    sv_sem, tk_send, tk_recv, row_send, row_recv, ring_send, ring_recv, tg_send, tg_recv,
):
    dp, row, col = lax.axis_index("dp"), lax.axis_index("row"), lax.axis_index("col")
    x, y = lax.rem(dp, X), lax.div(dp, X)
    core, z = lax.rem(col, 2), lax.div(col, 2)
    x_right = (y * X + lax.rem(x + 1, X), row, col)
    x_left = (y * X + lax.rem(x + X - 1, X), row, col)
    y_right = (lax.rem(y + 1, Y) * X + x, row, col)
    y_left = (lax.rem(y + Y - 1, Y) * X + x, row, col)
    row_right, row_left = (dp, row + 1, col), (dp, row - 1, col)
    sibling = (dp, row, z * 2 + 1 - core)
    z_right, z_left = lax.rem(z + 1, Z), lax.rem(z + Z - 1, Z)
    dev_z_right, dev_z_left = (dp, row, z_right * 2 + core), (dp, row, z_left * 2 + core)

    load = pltpu.make_async_copy(sv_hbm, sv.at[pl.ds(0, CAP)], sv_sem)
    load.start()

    barrier = pltpu.get_barrier_semaphore()
    at_x = lambda place: (y * X + place, row, col)
    at_y = lambda place: (place * X + x, row, col)
    peers = [at_y(lax.rem(y + o, Y)) for o in range(1, Y)] + [at_x(lax.rem(x + o, X)) for o in range(1, X)]
    for other in [dev_z_right, dev_z_left] + peers + [sibling]:
        pl.semaphore_signal(barrier, inc=1, device_id=other, device_id_type=MESH)

    @pl.when(row < R - 1)
    def _():
        pl.semaphore_signal(barrier, inc=1, device_id=row_right, device_id_type=MESH)

    @pl.when(row > 0)
    def _():
        pl.semaphore_signal(barrier, inc=1, device_id=row_left, device_id_type=MESH)

    own = tok_in[...].astype(F32)
    for p in range(BT // 2):
        pair = [own[:, (2 * p + i) * BLK : (2 * p + i + 1) * BLK] for i in range(2)]
        agb[col, pl.ds(3 * p, 3)] = jnp.concatenate(pair, 0).astype(BF16).reshape(3, 16, BLK)

    pl.semaphore_wait(barrier, X + Y + 1 + (row < R - 1).astype(jnp.int32) + (row > 0).astype(jnp.int32))

    def token_copy(slot, piece, send, device):
        half = pl.ds(9 * piece, 9)
        return pltpu.make_async_remote_copy(
            src_ref=agb.at[slot, half],
            dst_ref=agb.at[slot, half],
            send_sem=tk_send.at[piece, send],
            recv_sem=tk_recv.at[piece, slot],
            device_id=device,
            device_id_type=MESH,
        )

    for piece in range(2):
        token_copy(col, piece, 0, dev_z_right).start()
        token_copy(col, piece, 1, dev_z_left).start()
        token_copy(col, piece, 2, sibling).start()

    last_rows = cot_in[pl.ds(32, 4), :].astype(F32)
    for k in range(NC):
        for jj in range(NJ):
            j = k * NJ + jj
            cot[k, pl.ds(2 * jj, 2)] = cot_in[pl.ds(0, 32), pl.ds(j * BLK, BLK)].reshape(2, 16, BLK)
        cot[k, 2 * NJ] = jnp.concatenate(
            [last_rows[:, (k * NJ + jj) * BLK : (k * NJ + jj + 1) * BLK] for jj in range(NJ)], 0
        ).astype(BF16)
    sv[CAP] = jnp.zeros((BLK, COLS * BLK), BF16)
    rr[:, 0] = jnp.zeros((NC, 2 * NJ + 1, 16, BLK), BF16)
    rl[:, R - 1] = jnp.zeros((NC, 2 * NJ + 1, 16, BLK), BF16)
    tgacc[...] = jnp.zeros(tgacc.shape, F32)
    tok[BT] = jnp.zeros((TOK, BLK), BF16)
    tokt[BT] = jnp.zeros((BLK, 2 * BLK), BF16)

    from_left, from_right = z_left * 2 + core, z_right * 2 + core
    def unpack(p, carry):
        pieces = [agb[c, pl.ds(3 * p, 3)].astype(F32).reshape(48, BLK) for c in range(2 * Z)]
        for i in range(2):
            full = jnp.concatenate([v[24 * i : 24 * i + 24] for v in pieces], 0)
            ordered = jnp.concatenate(
                [full[36 * r : 36 * r + 32] for r in range(R)]
                + [full[36 * r + 32 : 36 * r + 36] for r in range(R)]
                + [jnp.zeros((2 * BLK - TOK, BLK), F32)],
                0,
            )
            tok[2 * p + i] = ordered[:TOK].astype(BF16)
            tokt[2 * p + i] = ordered.T.astype(BF16)
        return carry

    for piece in range(2):
        token_copy(from_left, piece, 0, dev_z_right).wait_recv()
        token_copy(from_left, piece, 3, sibling).start()
        token_copy(from_right, piece, 0, dev_z_left).wait_recv()
        token_copy(from_right, piece, 4, sibling).start()
        for other in range(Z):
            token_copy(other * 2 + 1 - core, piece, 2, sibling).wait_recv()
        lax.fori_loop(3 * piece, 3 * piece + 3, unpack, 0)
    for piece in range(2):
        for send in range(5):
            token_copy(col, piece, send, sibling).wait_send()
    load.wait()

    ring_ax = Ring(ta, ax1, ax2, X, x, x_right, x_left, ring_send, ring_recv, 0)
    direct_ay = Direct(ya, ay, Y, y, at_y, ring_send, ring_recv, 4)
    ring_by = Ring(tb, by1, by2, Y, y, y_right, y_left, ring_send, ring_recv, 11)
    direct_bx = Direct(xb, bx, X, x, at_x, ring_send, ring_recv, 19)

    def by_path(k, x_first, y_first):
        y_path = (k == 1) | (k == 4)

        @pl.when(y_path)
        def _():
            y_first()

        @pl.when(jnp.logical_not(y_path))
        def _():
            x_first()

    def columns(j):
        return pl.ds(pl.multiple_of(j * BLK, BLK), BLK)

    def row_sum_copy(k, dest, way):
        return pltpu.make_async_remote_copy(
            src_ref=part.at[k, dest],
            dst_ref=(rl if way else rr).at[k, dest],
            send_sem=row_send.at[lax.rem(k, 2), dest],
            recv_sem=row_recv.at[k, R * way + dest],
            device_id=row_left if way else row_right,
            device_id_type=MESH,
        )

    def row_sum_roles(step):
        return ((0, row == step - 1, range(R - 1, step - 1, -1)), (1, row == R - step, range(R - step)))

    def row_sum_drain(k, step):
        for way, mine, dests in row_sum_roles(step):

            @pl.when(mine)
            def _():
                for dest in dests:
                    row_sum_copy(k, dest, way).wait_send()

    def row_sum(k, step):
        for way, mine, dests in row_sum_roles(step):

            @pl.when(mine)
            def _():
                for dest in dests:
                    if step > 1:
                        row_sum_copy(k, dest, way).wait_recv()
                        got = (rl if way else rr)[k, dest].astype(F32)
                        part[k, dest] = (part[k, dest].astype(F32) + got).astype(BF16)
                    row_sum_copy(k, dest, way).start()

        if step > 1:
            row_sum_drain(k, step - 1)

    def gather_copy(k, source, step, way):
        return pltpu.make_async_remote_copy(
            src_ref=hg.at[k, source],
            dst_ref=hg.at[k, source],
            send_sem=row_send.at[lax.rem(k, 2), R + 2 * step + way],
            recv_sem=row_recv.at[k, 2 * R + source],
            device_id=row_right if way == 0 else row_left,
            device_id_type=MESH,
        )

    def gather_sources(step):
        return (
            (0, row - step, (row >= step), row < R - 1),
            (1, row + step, (row + step < R), row > 0),
        )

    def gather_drain(k, step):
        for way, source, have, onward in gather_sources(step):

            @pl.when(have & onward)
            def _():
                gather_copy(k, source, step, way).wait_send()

    def gather(k, step):
        for way, source, have, onward in gather_sources(step):
            if step > 0:

                @pl.when(have)
                def _():
                    gather_copy(k, source, step - 1, way).wait_recv()

            if step < R - 1:

                @pl.when(have & onward)
                def _():
                    gather_copy(k, source, step, way).start()

        if step > 0:
            gather_drain(k, step - 1)

    def forward(k):
        ends = []
        for jj in range(NJ):
            j = k * NJ + jj
            picked = jnp.concatenate([tok[rows[s, j]] for s in range(CAP)], 1)
            weight = sv[pl.ds(0, CAP), :, columns(j)].reshape(CAP * BLK, BLK)
            result = jnp.dot(picked, weight, preferred_element_type=F32)
            for d in range(R):
                part[k, d, pl.ds(2 * jj, 2)] = result[32 * d : 32 * d + 32].astype(BF16).reshape(2, 16, BLK)
            ends.append(result[32 * R :])
        for d in range(R):
            part[k, d, 2 * NJ] = jnp.concatenate([e[4 * d : 4 * d + 4] for e in ends], 0).astype(BF16)
        row_sum(k, 1)

    def activate(k):
        @pl.when(row > 0)
        def _():
            row_sum_copy(k, row, 0).wait_recv()

        @pl.when(row < R - 1)
        def _():
            row_sum_copy(k, row, 1).wait_recv()

        hidden = part[k, row].astype(F32) + rr[k, row].astype(F32) + rl[k, row].astype(F32)
        value, slope = gelu_pair(hidden)
        hg[k, row] = (cot[k].astype(F32) * slope).astype(BF16)
        gather(k, 0)
        act_out[k] = value.astype(BF16)
        row_sum_drain(k, R - 1)

    def grad_blocks(k):
        ends = [hg[k, s, 2 * NJ].astype(F32) for s in range(R)]
        blocks = []
        for jj in range(NJ):
            mains = [hg[k, s, pl.ds(2 * jj, 2)].reshape(32, BLK) for s in range(R)]
            end = jnp.concatenate([e[4 * jj : 4 * jj + 4] for e in ends], 0).astype(BF16)
            blocks.append(jnp.concatenate(mains + [end], 0))
        return blocks

    def weight_grad(k):
        blocks = grad_blocks(k)
        terms = []
        for jj in range(NJ):
            j = k * NJ + jj
            picked = jnp.concatenate([tokt[rows[s, j]] for s in range(CAP)], 0)
            grad = jnp.concatenate([blocks[jj], jnp.zeros((2 * BLK - TOK, BLK), BF16)], 0)
            term = jnp.dot(picked, grad, preferred_element_type=F32)
            terms.append(term.astype(BF16).reshape(Y, X, 16, BLK))

        def x_first():
            for jj in range(NJ):
                for xx in range(X):
                    ta[k, xx, :, jj] = terms[jj][:, xx]
            ring_ax.advance(k, 1)

        def y_first():
            for jj in range(NJ):
                tb[k, :, :, jj] = terms[jj]
            ring_by.advance(k, 1)

        by_path(k, x_first, y_first)
        for jj in range(NJ):
            grad = jnp.concatenate([blocks[jj].astype(F32), jnp.zeros((2 * BLK - TOK, BLK), F32)], 0)
            hgt[pl.ds(jj * BLK, BLK), :] = grad.T.astype(BF16)

    def token_grad(k):
        grad = hgt[...]

        def pair(p, carry):
            weights = [
                jnp.concatenate(
                    [sv[inv[2 * p + i, k * NJ + jj], :, columns(k * NJ + jj)] for jj in range(NJ)],
                    1,
                )
                for i in range(2)
            ]
            tgacc[p] += jnp.dot(jnp.concatenate(weights, 0), grad, preferred_element_type=F32)
            return carry

        lax.fori_loop(0, BT // 2, pair, 0, unroll=True)

    def tg_copy(step):
        if step == 0:
            src, dst, device = tgs.at[1 - core], tgr1, sibling
        elif step == 1:
            src, dst, device = tgs.at[core, z_right], tgr2.at[0], dev_z_right
        else:
            src, dst, device = tgs.at[core, z_left], tgr2.at[1], dev_z_left
        return pltpu.make_async_remote_copy(
            src_ref=src,
            dst_ref=dst,
            send_sem=tg_send.at[step],
            recv_sem=tg_recv.at[step],
            device_id=device,
            device_id_type=MESH,
        )

    def tg_first():
        def pair(p, carry):
            both = tgacc[p].T
            pieces = []
            for i in range(2):
                v = both[:, i * BLK : (i + 1) * BLK]
                order = []
                for r in range(R):
                    order += [v[32 * r : 32 * r + 32], v[32 * R + 4 * r : 32 * R + 4 * r + 4]]
                pieces.append(jnp.concatenate(order, 0))
            for c in range(2 * Z):
                shard = jnp.concatenate([v[24 * c : 24 * c + 24] for v in pieces], 0)
                tgs[c % 2, c // 2, pl.ds(3 * p, 3)] = shard.astype(BF16).reshape(3, 16, BLK)
            return carry

        lax.fori_loop(0, BT // 2, pair, 0)
        tg_copy(0).start()

    def tg_second():
        tg_copy(0).wait_recv()
        tgs[core] = (tgs[core].astype(F32) + tgr1[...].astype(F32)).astype(BF16)
        tg_copy(1).start()
        tg_copy(2).start()
        tg_copy(0).wait_send()

    def tg_last():
        tg_copy(1).wait_recv()
        tg_copy(2).wait_recv()
        total = tgs[core, z].astype(F32) + tgr2[0].astype(F32) + tgr2[1].astype(F32)
        tg_out[...] = total.astype(BF16)
        tg_copy(1).wait_send()
        tg_copy(2).wait_send()

    factor = float(TOK * X * Y) ** (-0.5)

    def write(k, total):
        for jj in range(NJ):
            sg_out[:, columns(k * NJ + jj)] = total[jj] * factor

    def sums_2(k):
        by_path(k, lambda: ring_ax.advance(k, 2), lambda: ring_by.advance(k, 2))

    def sums_3(k):
        def x_first():
            ya[k] = ring_ax.finish(k).astype(BF16)
            direct_ay.start(k)

        by_path(k, x_first, lambda: ring_by.advance(k, 3))

    def sums_4(k):
        def x_first():
            write(k, direct_ay.finish(k))
            direct_ay.drain(k)

        by_path(k, x_first, lambda: ring_by.advance(k, 4))

    def sums_5(k):
        def y_first():
            xb[k] = ring_by.finish(k).astype(BF16)
            direct_bx.start(k)

        by_path(k, lambda: None, y_first)

    def sums_6(k):
        def y_first():
            write(k, direct_bx.finish(k))
            direct_bx.drain(k)

        by_path(k, lambda: None, y_first)

    stages = (
        (6, lambda k: gather(k, 3)),
        (5, lambda k: gather(k, 2)),
        (4, lambda k: gather(k, 1)),
        (3, activate),
        (2, lambda k: row_sum(k, 3)),
        (1, lambda k: row_sum(k, 2)),
        (11, sums_6),
        (10, sums_5),
        (9, sums_4),
        (8, sums_3),
        (7, sums_2),
        (6, weight_grad),
        (0, forward),
        (6, token_grad),
    )

    def tick(t, carry):
        for stage, work in stages:
            k = t - stage * LAG

            @pl.when((k >= 0) & (k < NC))
            def _():
                work(k)

        for stage, work in ((6, tg_first), (7, tg_second)):

            @pl.when(t == NC - 1 + stage * LAG)
            def _():
                work()

        return carry

    lax.fori_loop(0, max(NC + 9 * LAG, 5 + 11 * LAG), tick, 0)
    tg_last()


def body(tokens_in, slot_values, slot_rows, act_cotangent):
    blocks = jnp.arange(BT, dtype=jnp.int32)
    slots = jnp.arange(CAP, dtype=jnp.int32)
    match = slot_rows[None, :, :] == blocks[:, None, None]
    inverse = jnp.min(jnp.where(match, slots[None, :, None], CAP), axis=1)

    def dma(*shape):
        return pltpu.SemaphoreType.DMA(shape)

    def buf(*shape, dtype=BF16):
        return pltpu.VMEM(shape, dtype)

    vmem = pl.BlockSpec(memory_space=pltpu.VMEM)
    smem = pl.BlockSpec(memory_space=pltpu.SMEM)
    tiles = 2 * NJ + 1
    packed, grad, summed = pl.pallas_call(
        kernel,
        out_shape=(
            jax.ShapeDtypeStruct((NC, tiles, 16, BLK), BF16),
            jax.ShapeDtypeStruct((18, 16, BLK), BF16),
            jax.ShapeDtypeStruct((16, COLS * BLK), F32),
        ),
        in_specs=[vmem, smem, smem, vmem, pl.BlockSpec(memory_space=pl.ANY)],
        out_specs=(vmem, vmem, vmem),
        scratch_shapes=[
            buf(2 * Z, 18, 16, BLK),
            buf(BT + 1, TOK, BLK),
            buf(BT + 1, BLK, 2 * BLK),
            buf(CAP + 1, BLK, COLS * BLK),
            buf(NC, tiles, 16, BLK),
            buf(NC, R, tiles, 16, BLK),
            buf(NC, R, tiles, 16, BLK),
            buf(NC, R, tiles, 16, BLK),
            buf(NC, R, tiles, 16, BLK),
            buf(NC, X, Y, NJ, 16, BLK),
            buf(NC, 2, Y // 2, NJ, 16, BLK),
            buf(NC, 1, 2, Y, NJ, 16, BLK),
            buf(NC, Y, NJ, 16, BLK),
            buf(NC, Y - 1, NJ, 16, BLK),
            buf(NC, Y, X, NJ, 16, BLK),
            buf(NC, 2, X // 2, NJ, 16, BLK),
            buf(NC, 3, 2, X, NJ, 16, BLK),
            buf(NC, X, NJ, 16, BLK),
            buf(NC, X - 1, NJ, 16, BLK),
            buf(NJ * BLK, 2 * BLK),
            buf(BT // 2, 2 * BLK, 2 * BLK, dtype=F32),
            buf(2, Z, 18, 16, BLK),
            buf(Z, 18, 16, BLK),
            buf(2, 18, 16, BLK),
            pltpu.SemaphoreType.DMA,
            dma(2, 5),
            dma(2, 2 * Z),
            dma(2, R + 6),
            dma(NC, 3 * R),
            dma(2, 22),
            dma(NC, 22),
            dma(3),
            dma(3),
        ],
        compiler_params=pltpu.CompilerParams(
            collective_id=0, has_side_effects=True, vmem_limit_bytes=52 * 1024 * 1024
        ),
    )(tokens_in, slot_rows, inverse, act_cotangent, slot_values.reshape(CAP, BLK, COLS * BLK))

    mains = packed[:, : 2 * NJ].reshape(NC, NJ, 32, BLK)
    ends = packed[:, 2 * NJ].reshape(NC, NJ, 4, BLK)
    activation = jnp.concatenate([mains, ends], axis=2).transpose(2, 0, 1, 3).reshape(36, COLS * BLK)
    token_grad = grad.reshape(BT // 2, 2, 24, BLK).transpose(2, 0, 1, 3).reshape(24, BT * BLK)
    slot_grad = summed.reshape(16, 1, COLS * BLK)
    return (activation, token_grad, slot_grad)


def solution(mesh):
    return jax.shard_map(
        body,
        mesh=mesh,
        in_specs=(
            P(("dp", "col"), "row"),
            P("row", "col"),
            P("row", "col"),
            P(("dp", "row"), "col"),
        ),
        out_specs=(P(("dp", "row"), "col"), P(("dp", "col"), "row"), P("dp", "row", "col")),
        check_vma=False,
    )
```

```python
import functools

import jax
import jax.numpy as jnp
from jax import lax
from jax.experimental import pallas as pl
from jax.experimental.pallas import tpu as pltpu
from jax.sharding import PartitionSpec as P

MESH = pl.DeviceIdType.MESH
BF16 = jnp.bfloat16
F32 = jnp.float32

BLK = 128
CAP = 4
BT = 12
COLS = 32
X, Y = 4, 8
R = 4
Z = 3
TOK = 144
NC = 8
NJ = COLS // NC
LAG = 1
X_FIRST = (2, 4, 7)
Y_FIRST = (2, 4, 6, 8, 11)
Y_CHUNKS = (0, 3)
SLOTS = 4

root_two_pi = 0.7978845608028654
cubic_coef = 0.044715


def gelu_pair(hidden):
    inner = root_two_pi * (hidden + cubic_coef * hidden * hidden * hidden)
    tangent = jnp.tanh(inner)
    value = 0.5 * hidden * (1.0 + tangent)
    slope = 0.5 * (1.0 + tangent) + 0.5 * hidden * (1.0 - tangent * tangent) * root_two_pi * (
        1.0 + 3.0 * cubic_coef * hidden * hidden
    )
    return (value, slope)


class Ring:
    def __init__(self, total, first, later, size, here, right, left, send, recv, base):
        self.total, self.first, self.later = total, first, later
        self.size, self.here, self.right, self.left = size, here, right, left
        self.send, self.recv, self.base = send, recv, base
        self.half = size // 2

    def shard(self, k, step, way):
        offset = self.half + 1 - step
        place = lax.rem(self.here + (offset if way == 0 else self.size - offset), self.size)
        ref = self.total.at[k, place]
        if step == 1:
            part = self.total.shape[2] // 2
            return ref.at[pl.ds(way * part, part)]
        return ref

    def landing(self, k, step, way):
        return self.first.at[k, way] if step == 1 else self.later.at[k, step - 2, way]

    def copy(self, k, step, way):
        kind = self.base + 2 * (step - 1) + way
        return pltpu.make_async_remote_copy(
            src_ref=self.shard(k, step, way),
            dst_ref=self.landing(k, step, way),
            send_sem=self.send.at[lax.rem(k, SLOTS), kind],
            recv_sem=self.recv.at[k, kind],
            device_id=self.right if way == 0 else self.left,
            device_id_type=MESH,
        )

    def drain(self, k, step):
        for way in range(2):
            self.copy(k, step, way).wait_send()

    def advance(self, k, step):
        for way in range(2):
            if step > 1:
                self.copy(k, step - 1, way).wait_recv()
                ref = self.shard(k, step, way)
                if step == 2:
                    part = self.total.shape[2] // 2
                    ref = ref.at[pl.ds(way * part, part)]
                got = self.landing(k, step - 1, way)
                ref[...] = (ref[...].astype(F32) + got[...].astype(F32)).astype(BF16)
            self.copy(k, step, way).start()
        if step > 1:
            self.drain(k, step - 1)

    def finish(self, k):
        last = self.half
        for way in range(2):
            self.copy(k, last, way).wait_recv()
        result = self.total[k, self.here].astype(F32)
        result = result + self.landing(k, last, 0)[...].astype(F32)
        result = result + self.landing(k, last, 1)[...].astype(F32)
        self.drain(k, last)
        return result


class Direct:
    def __init__(self, total, landing, size, here, device, send, recv, base):
        self.total, self.landing, self.size, self.here = total, landing, size, here
        self.device, self.send, self.recv, self.base = device, send, recv, base

    def copy(self, k, offset):
        place = lax.rem(self.here + offset, self.size)
        kind = self.base + offset - 1
        return pltpu.make_async_remote_copy(
            src_ref=self.total.at[k, place],
            dst_ref=self.landing.at[k, offset - 1],
            send_sem=self.send.at[lax.rem(k, SLOTS), kind],
            recv_sem=self.recv.at[k, kind],
            device_id=self.device(place),
            device_id_type=MESH,
        )

    def start(self, k):
        far_first = sorted(range(1, self.size), key=lambda o: -min(o, self.size - o))
        for offset in far_first:
            self.copy(k, offset).start()

    def drain(self, k):
        for offset in range(1, self.size):
            self.copy(k, offset).wait_send()

    def finish(self, k):
        for offset in range(1, self.size):
            self.copy(k, offset).wait_recv()
        result = self.total[k, self.here].astype(F32)
        for offset in range(1, self.size):
            result = result + self.landing[k, offset - 1].astype(F32)
        return result


def kernel(
    tok_in, table, cot_in, sv_hbm,
    act_out, tg_out, sg_out,
    agb, tok, tokt, sv, cot, part, rr, rl, hg,
    ta, ax1, ax2, ya, ay, tb, by1, by2, xb, bx,
    hgt, tgacc, tgs, tgr1, tgr2,
    sv_sem, tk_send, tk_recv, row_send, row_recv, ring_send, ring_recv, tg_send, tg_recv,
):
    dp, row, col = lax.axis_index("dp"), lax.axis_index("row"), lax.axis_index("col")
    x, y = lax.rem(dp, X), lax.div(dp, X)
    core, z = lax.rem(col, 2), lax.div(col, 2)
    x_right = (y * X + lax.rem(x + 1, X), row, col)
    x_left = (y * X + lax.rem(x + X - 1, X), row, col)
    y_right = (lax.rem(y + 1, Y) * X + x, row, col)
    y_left = (lax.rem(y + Y - 1, Y) * X + x, row, col)
    row_right, row_left = (dp, row + 1, col), (dp, row - 1, col)
    sibling = (dp, row, z * 2 + 1 - core)
    z_right, z_left = lax.rem(z + 1, Z), lax.rem(z + Z - 1, Z)
    dev_z_right, dev_z_left = (dp, row, z_right * 2 + core), (dp, row, z_left * 2 + core)

    load = pltpu.make_async_copy(sv_hbm, sv.at[pl.ds(0, CAP)], sv_sem)
    load.start()

    barrier = pltpu.get_barrier_semaphore()
    at_x = lambda place: (y * X + place, row, col)
    at_y = lambda place: (place * X + x, row, col)
    peers = [at_y(lax.rem(y + o, Y)) for o in range(1, Y)] + [at_x(lax.rem(x + o, X)) for o in range(1, X)]
    for other in [dev_z_right, dev_z_left] + peers + [sibling]:
        pl.semaphore_signal(barrier, inc=1, device_id=other, device_id_type=MESH)

    @pl.when(row < R - 1)
    def _():
        pl.semaphore_signal(barrier, inc=1, device_id=row_right, device_id_type=MESH)

    @pl.when(row > 0)
    def _():
        pl.semaphore_signal(barrier, inc=1, device_id=row_left, device_id_type=MESH)

    own = tok_in[...].astype(F32)
    for p in range(BT // 2):
        pair = [own[:, (2 * p + i) * BLK : (2 * p + i + 1) * BLK] for i in range(2)]
        agb[col, pl.ds(3 * p, 3)] = jnp.concatenate(pair, 0).astype(BF16).reshape(3, 16, BLK)

    pl.semaphore_wait(barrier, X + Y + 1 + (row < R - 1).astype(jnp.int32) + (row > 0).astype(jnp.int32))

    def token_copy(slot, piece, send, device):
        half = pl.ds(9 * piece, 9)
        return pltpu.make_async_remote_copy(
            src_ref=agb.at[slot, half],
            dst_ref=agb.at[slot, half],
            send_sem=tk_send.at[piece, send],
            recv_sem=tk_recv.at[piece, slot],
            device_id=device,
            device_id_type=MESH,
        )

    for piece in range(2):
        token_copy(col, piece, 0, dev_z_right).start()
        token_copy(col, piece, 1, dev_z_left).start()
        token_copy(col, piece, 2, sibling).start()

    last_rows = cot_in[pl.ds(32, 4), :].astype(F32)
    for k in range(NC):
        for jj in range(NJ):
            j = k * NJ + jj
            cot[k, pl.ds(2 * jj, 2)] = cot_in[pl.ds(0, 32), pl.ds(j * BLK, BLK)].reshape(2, 16, BLK)
        cot[k, 2 * NJ] = jnp.concatenate(
            [last_rows[:, (k * NJ + jj) * BLK : (k * NJ + jj + 1) * BLK] for jj in range(NJ)], 0
        ).astype(BF16)
    sv[CAP] = jnp.zeros((BLK, COLS * BLK), BF16)
    rr[:, 0] = jnp.zeros((NC, 2 * NJ + 1, 16, BLK), BF16)
    rl[:, R - 1] = jnp.zeros((NC, 2 * NJ + 1, 16, BLK), BF16)
    tgacc[...] = jnp.zeros(tgacc.shape, F32)
    tok[BT] = jnp.zeros((TOK, BLK), BF16)
    tokt[BT] = jnp.zeros((BLK, 2 * BLK), BF16)

    from_left, from_right = z_left * 2 + core, z_right * 2 + core
    def unpack(p, carry):
        pieces = [agb[c, pl.ds(3 * p, 3)].astype(F32).reshape(48, BLK) for c in range(2 * Z)]
        for i in range(2):
            full = jnp.concatenate([v[24 * i : 24 * i + 24] for v in pieces], 0)
            ordered = jnp.concatenate(
                [full[36 * r : 36 * r + 32] for r in range(R)]
                + [full[36 * r + 32 : 36 * r + 36] for r in range(R)]
                + [jnp.zeros((2 * BLK - TOK, BLK), F32)],
                0,
            )
            tok[2 * p + i] = ordered[:TOK].astype(BF16)
            tokt[2 * p + i] = ordered.T.astype(BF16)
        return carry

    for piece in range(2):
        token_copy(from_left, piece, 0, dev_z_right).wait_recv()
        token_copy(from_left, piece, 3, sibling).start()
        token_copy(from_right, piece, 0, dev_z_left).wait_recv()
        token_copy(from_right, piece, 4, sibling).start()
        for other in range(Z):
            token_copy(other * 2 + 1 - core, piece, 2, sibling).wait_recv()
        lax.fori_loop(3 * piece, 3 * piece + 3, unpack, 0)
    for piece in range(2):
        for send in range(5):
            token_copy(col, piece, send, sibling).wait_send()
    load.wait()

    ring_ax = Ring(ta, ax1, ax2, X, x, x_right, x_left, ring_send, ring_recv, 0)
    direct_ay = Direct(ya, ay, Y, y, at_y, ring_send, ring_recv, 4)
    ring_by = Ring(tb, by1, by2, Y, y, y_right, y_left, ring_send, ring_recv, 11)
    direct_bx = Direct(xb, bx, X, x, at_x, ring_send, ring_recv, 19)

    def by_path(k, x_first, y_first):
        y_path = functools.reduce(jnp.logical_or, [k == chunk for chunk in Y_CHUNKS])

        @pl.when(y_path)
        def _():
            y_first()

        @pl.when(jnp.logical_not(y_path))
        def _():
            x_first()

    def columns(j):
        return pl.ds(pl.multiple_of(j * BLK, BLK), BLK)

    def row_sum_copy(k, dest, way):
        return pltpu.make_async_remote_copy(
            src_ref=part.at[k, dest],
            dst_ref=(rl if way else rr).at[k, dest],
            send_sem=row_send.at[lax.rem(k, SLOTS), dest],
            recv_sem=row_recv.at[k, R * way + dest],
            device_id=row_left if way else row_right,
            device_id_type=MESH,
        )

    def row_sum_roles(step):
        return ((0, row == step - 1, range(R - 1, step - 1, -1)), (1, row == R - step, range(R - step)))

    def row_sum_drain(k, step):
        for way, mine, dests in row_sum_roles(step):

            @pl.when(mine)
            def _():
                for dest in dests:
                    row_sum_copy(k, dest, way).wait_send()

    def row_sum(k, step):
        for way, mine, dests in row_sum_roles(step):

            @pl.when(mine)
            def _():
                for dest in dests:
                    if step > 1:
                        row_sum_copy(k, dest, way).wait_recv()
                        got = (rl if way else rr)[k, dest].astype(F32)
                        part[k, dest] = (part[k, dest].astype(F32) + got).astype(BF16)
                    row_sum_copy(k, dest, way).start()

        if step > 1:
            row_sum_drain(k, step - 1)

    def gather_copy(k, source, step, way):
        return pltpu.make_async_remote_copy(
            src_ref=hg.at[k, source],
            dst_ref=hg.at[k, source],
            send_sem=row_send.at[lax.rem(k, SLOTS), R + 2 * step + way],
            recv_sem=row_recv.at[k, 2 * R + source],
            device_id=row_right if way == 0 else row_left,
            device_id_type=MESH,
        )

    def gather_sources(step):
        return (
            (0, row - step, (row >= step), row < R - 1),
            (1, row + step, (row + step < R), row > 0),
        )

    def gather_drain(k, step):
        for way, source, have, onward in gather_sources(step):

            @pl.when(have & onward)
            def _():
                gather_copy(k, source, step, way).wait_send()

    def gather(k, step):
        for way, source, have, onward in gather_sources(step):
            if step > 0:

                @pl.when(have)
                def _():
                    gather_copy(k, source, step - 1, way).wait_recv()

            if step < R - 1:

                @pl.when(have & onward)
                def _():
                    gather_copy(k, source, step, way).start()

        if step > 0:
            gather_drain(k, step - 1)

    def forward(k):
        ends = []
        for jj in range(NJ):
            j = k * NJ + jj
            picked = jnp.concatenate([tok[table[s, j]] for s in range(CAP)], 1)
            weight = sv[pl.ds(0, CAP), :, columns(j)].reshape(CAP * BLK, BLK)
            result = jnp.dot(picked, weight, preferred_element_type=F32)
            for d in range(R):
                part[k, d, pl.ds(2 * jj, 2)] = result[32 * d : 32 * d + 32].astype(BF16).reshape(2, 16, BLK)
            ends.append(result[32 * R :])
        for d in range(R):
            part[k, d, 2 * NJ] = jnp.concatenate([e[4 * d : 4 * d + 4] for e in ends], 0).astype(BF16)
        row_sum(k, 1)

    def activate(k):
        @pl.when(row > 0)
        def _():
            row_sum_copy(k, row, 0).wait_recv()

        @pl.when(row < R - 1)
        def _():
            row_sum_copy(k, row, 1).wait_recv()

        hidden = part[k, row].astype(F32) + rr[k, row].astype(F32) + rl[k, row].astype(F32)
        value, slope = gelu_pair(hidden)
        hg[k, row] = (cot[k].astype(F32) * slope).astype(BF16)
        gather(k, 0)
        act_out[k] = value.astype(BF16)
        row_sum_drain(k, R - 1)

    def grad_blocks(k):
        ends = [hg[k, s, 2 * NJ].astype(F32) for s in range(R)]
        blocks = []
        for jj in range(NJ):
            mains = [hg[k, s, pl.ds(2 * jj, 2)].reshape(32, BLK) for s in range(R)]
            end = jnp.concatenate([e[4 * jj : 4 * jj + 4] for e in ends], 0).astype(BF16)
            blocks.append(jnp.concatenate(mains + [end], 0))
        return blocks

    def weight_grad(k):
        blocks = grad_blocks(k)
        terms = []
        for jj in range(NJ):
            j = k * NJ + jj
            picked = jnp.concatenate([tokt[table[s, j]] for s in range(CAP)], 0)
            grad = jnp.concatenate([blocks[jj], jnp.zeros((2 * BLK - TOK, BLK), BF16)], 0)
            term = jnp.dot(picked, grad, preferred_element_type=F32)
            terms.append(term.astype(BF16).reshape(Y, X, 16, BLK))

        def x_first():
            for jj in range(NJ):
                for xx in range(X):
                    ta[k, xx, :, jj] = terms[jj][:, xx]
            ring_ax.advance(k, 1)

        def y_first():
            for jj in range(NJ):
                tb[k, :, :, jj] = terms[jj]
            ring_by.advance(k, 1)

        by_path(k, x_first, y_first)
        for jj in range(NJ):
            grad = jnp.concatenate([blocks[jj].astype(F32), jnp.zeros((2 * BLK - TOK, BLK), F32)], 0)
            hgt[pl.ds(jj * BLK, BLK), :] = grad.T.astype(BF16)

    def token_grad(k):
        grad = hgt[...]

        def pair(p, carry):
            weights = [
                jnp.concatenate(
                    [sv[table[CAP + 2 * p + i, k * NJ + jj], :, columns(k * NJ + jj)] for jj in range(NJ)],
                    1,
                )
                for i in range(2)
            ]
            tgacc[p] += jnp.dot(jnp.concatenate(weights, 0), grad, preferred_element_type=F32)
            return carry

        lax.fori_loop(0, BT // 2, pair, 0, unroll=True)

    def tg_copy(step):
        if step == 0:
            src, dst, device = tgs.at[1 - core], tgr1, sibling
        elif step == 1:
            src, dst, device = tgs.at[core, z_right], tgr2.at[0], dev_z_right
        else:
            src, dst, device = tgs.at[core, z_left], tgr2.at[1], dev_z_left
        return pltpu.make_async_remote_copy(
            src_ref=src,
            dst_ref=dst,
            send_sem=tg_send.at[step],
            recv_sem=tg_recv.at[step],
            device_id=device,
            device_id_type=MESH,
        )

    def tg_first():
        def pair(p, carry):
            both = tgacc[p].T
            pieces = []
            for i in range(2):
                v = both[:, i * BLK : (i + 1) * BLK]
                order = []
                for r in range(R):
                    order += [v[32 * r : 32 * r + 32], v[32 * R + 4 * r : 32 * R + 4 * r + 4]]
                pieces.append(jnp.concatenate(order, 0))
            for c in range(2 * Z):
                shard = jnp.concatenate([v[24 * c : 24 * c + 24] for v in pieces], 0)
                tgs[c % 2, c // 2, pl.ds(3 * p, 3)] = shard.astype(BF16).reshape(3, 16, BLK)
            return carry

        lax.fori_loop(0, BT // 2, pair, 0)
        tg_copy(0).start()

    def tg_second():
        tg_copy(0).wait_recv()
        tgs[core] = (tgs[core].astype(F32) + tgr1[...].astype(F32)).astype(BF16)
        tg_copy(1).start()
        tg_copy(2).start()
        tg_copy(0).wait_send()

    def tg_last():
        tg_copy(1).wait_recv()
        tg_copy(2).wait_recv()
        total = tgs[core, z].astype(F32) + tgr2[0].astype(F32) + tgr2[1].astype(F32)
        tg_out[...] = total.astype(BF16)
        tg_copy(1).wait_send()
        tg_copy(2).wait_send()

    factor = float(TOK * X * Y) ** (-0.5)

    def write(k, total):
        for jj in range(NJ):
            sg_out[:, columns(k * NJ + jj)] = total[jj] * factor

    def x_last(k):
        ya[k] = ring_ax.finish(k).astype(BF16)
        direct_ay.start(k)

    def x_first_sum(k):
        write(k, direct_ay.finish(k))
        direct_ay.drain(k)

    def y_last(k):
        xb[k] = ring_by.finish(k).astype(BF16)
        direct_bx.start(k)

    def y_first_sum(k):
        write(k, direct_bx.finish(k))
        direct_bx.drain(k)

    def only_x(work):
        return lambda k: by_path(k, lambda: work(k), lambda: None)

    def only_y(work):
        return lambda k: by_path(k, lambda: None, lambda: work(k))

    ready = 6 * LAG
    stages = (
        (5 * LAG, lambda k: gather(k, 2)),
        (4 * LAG, lambda k: gather(k, 1)),
        (3 * LAG, activate),
        (2 * LAG, lambda k: row_sum(k, 3)),
        (LAG, lambda k: row_sum(k, 2)),
        (ready + X_FIRST[0], only_x(lambda k: ring_ax.advance(k, 2))),
        (ready + Y_FIRST[2], only_y(lambda k: ring_by.advance(k, 4))),
        (ready + Y_FIRST[1], only_y(lambda k: ring_by.advance(k, 3))),
        (ready + Y_FIRST[0], only_y(lambda k: ring_by.advance(k, 2))),
        (ready + X_FIRST[1], only_x(x_last)),
        (ready + Y_FIRST[3], only_y(y_last)),
        (ready, lambda k: gather(k, 3)),
        (ready, weight_grad),
        (0, forward),
        (ready, token_grad),
        (ready + X_FIRST[2], only_x(x_first_sum)),
        (ready + Y_FIRST[4], only_y(y_first_sum)),
    )

    def tick(t, carry):
        for stage, work in stages:
            k = t - stage

            @pl.when((k >= 0) & (k < NC))
            def _():
                work(k)

        for stage, work in ((ready, tg_first), (ready + X_FIRST[0], tg_second)):

            @pl.when(t == NC - 1 + stage)
            def _():
                work()

        return carry

    ticks = max(NC + ready + X_FIRST[2], Y_CHUNKS[-1] + 1 + ready + Y_FIRST[4])
    lax.fori_loop(0, ticks, tick, 0)
    tg_last()


def body(tokens_in, slot_values, slot_rows, act_cotangent):
    blocks = jnp.arange(BT, dtype=jnp.int32)
    slots = jnp.arange(CAP, dtype=jnp.int32)
    match = slot_rows[None, :, :] == blocks[:, None, None]
    inverse = jnp.min(jnp.where(match, slots[None, :, None], CAP), axis=1)
    table = jnp.concatenate([slot_rows, inverse], axis=0)

    def dma(*shape):
        return pltpu.SemaphoreType.DMA(shape)

    def buf(*shape, dtype=BF16):
        return pltpu.VMEM(shape, dtype)

    vmem = pl.BlockSpec(memory_space=pltpu.VMEM)
    smem = pl.BlockSpec(memory_space=pltpu.SMEM)
    tiles = 2 * NJ + 1
    packed, grad, summed = pl.pallas_call(
        kernel,
        out_shape=(
            jax.ShapeDtypeStruct((NC, tiles, 16, BLK), BF16),
            jax.ShapeDtypeStruct((18, 16, BLK), BF16),
            jax.ShapeDtypeStruct((16, COLS * BLK), F32),
        ),
        in_specs=[vmem, smem, vmem, pl.BlockSpec(memory_space=pl.ANY)],
        out_specs=(vmem, vmem, vmem),
        scratch_shapes=[
            buf(2 * Z, 18, 16, BLK),
            buf(BT + 1, TOK, BLK),
            buf(BT + 1, BLK, 2 * BLK),
            buf(CAP + 1, BLK, COLS * BLK),
            buf(NC, tiles, 16, BLK),
            buf(NC, R, tiles, 16, BLK),
            buf(NC, R, tiles, 16, BLK),
            buf(NC, R, tiles, 16, BLK),
            buf(NC, R, tiles, 16, BLK),
            buf(NC, X, Y, NJ, 16, BLK),
            buf(NC, 2, Y // 2, NJ, 16, BLK),
            buf(NC, 1, 2, Y, NJ, 16, BLK),
            buf(NC, Y, NJ, 16, BLK),
            buf(NC, Y - 1, NJ, 16, BLK),
            buf(NC, Y, X, NJ, 16, BLK),
            buf(NC, 2, X // 2, NJ, 16, BLK),
            buf(NC, 3, 2, X, NJ, 16, BLK),
            buf(NC, X, NJ, 16, BLK),
            buf(NC, X - 1, NJ, 16, BLK),
            buf(NJ * BLK, 2 * BLK),
            buf(BT // 2, 2 * BLK, 2 * BLK, dtype=F32),
            buf(2, Z, 18, 16, BLK),
            buf(Z, 18, 16, BLK),
            buf(2, 18, 16, BLK),
            pltpu.SemaphoreType.DMA,
            dma(2, 5),
            dma(2, 2 * Z),
            dma(SLOTS, R + 6),
            dma(NC, 3 * R),
            dma(SLOTS, 22),
            dma(NC, 22),
            dma(3),
            dma(3),
        ],
        compiler_params=pltpu.CompilerParams(
            collective_id=0, has_side_effects=True, vmem_limit_bytes=52 * 1024 * 1024
        ),
    )(tokens_in, table, act_cotangent, slot_values.reshape(CAP, BLK, COLS * BLK))

    mains = packed[:, : 2 * NJ].reshape(NC, NJ, 32, BLK)
    ends = packed[:, 2 * NJ].reshape(NC, NJ, 4, BLK)
    activation = jnp.concatenate([mains, ends], axis=2).transpose(2, 0, 1, 3).reshape(36, COLS * BLK)
    token_grad = grad.reshape(BT // 2, 2, 24, BLK).transpose(2, 0, 1, 3).reshape(24, BT * BLK)
    slot_grad = summed.reshape(16, 1, COLS * BLK)
    return (activation, token_grad, slot_grad)


def solution(mesh):
    return jax.shard_map(
        body,
        mesh=mesh,
        in_specs=(
            P(("dp", "col"), "row"),
            P("row", "col"),
            P("row", "col"),
            P(("dp", "row"), "col"),
        ),
        out_specs=(P(("dp", "row"), "col"), P(("dp", "col"), "row"), P("dp", "row", "col")),
        check_vma=False,
    )
```

```python
import functools

import jax
import jax.numpy as jnp
from jax import lax
from jax.experimental import pallas as pl
from jax.experimental.pallas import tpu as pltpu
from jax.sharding import PartitionSpec as P

MESH = pl.DeviceIdType.MESH
BF16 = jnp.bfloat16
F32 = jnp.float32

BLK = 128
CAP = 4
BT = 12
COLS = 32
X, Y = 4, 8
R = 4
Z = 3
TOK = 144
NC = 8
NJ = COLS // NC
LAG = 1
X_FIRST = (2, 4, 7)
Y_FIRST = (2, 4, 6, 8, 11)
Y_CHUNKS = (0, 3)
SLOTS = 4

root_two_pi = 0.7978845608028654
cubic_coef = 0.044715


def gelu_pair(hidden):
    inner = root_two_pi * (hidden + cubic_coef * hidden * hidden * hidden)
    tangent = jnp.tanh(inner)
    value = 0.5 * hidden * (1.0 + tangent)
    slope = 0.5 * (1.0 + tangent) + 0.5 * hidden * (1.0 - tangent * tangent) * root_two_pi * (
        1.0 + 3.0 * cubic_coef * hidden * hidden
    )
    return (value, slope)


class Ring:
    def __init__(self, total, first, later, size, here, right, left, send, recv, base):
        self.total, self.first, self.later = total, first, later
        self.size, self.here, self.right, self.left = size, here, right, left
        self.send, self.recv, self.base = send, recv, base
        self.half = size // 2

    def shard(self, k, step, way):
        offset = self.half + 1 - step
        place = lax.rem(self.here + (offset if way == 0 else self.size - offset), self.size)
        ref = self.total.at[k, place]
        if step == 1:
            part = self.total.shape[2] // 2
            return ref.at[pl.ds(way * part, part)]
        return ref

    def landing(self, k, step, way):
        return self.first.at[k, way] if step == 1 else self.later.at[k, step - 2, way]

    def copy(self, k, step, way):
        kind = self.base + 2 * (step - 1) + way
        return pltpu.make_async_remote_copy(
            src_ref=self.shard(k, step, way),
            dst_ref=self.landing(k, step, way),
            send_sem=self.send.at[lax.rem(k, SLOTS), kind],
            recv_sem=self.recv.at[k, kind],
            device_id=self.right if way == 0 else self.left,
            device_id_type=MESH,
        )

    def drain(self, k, step):
        for way in range(2):
            self.copy(k, step, way).wait_send()

    def advance(self, k, step):
        for way in range(2):
            if step > 1:
                self.copy(k, step - 1, way).wait_recv()
                ref = self.shard(k, step, way)
                if step == 2:
                    part = self.total.shape[2] // 2
                    ref = ref.at[pl.ds(way * part, part)]
                got = self.landing(k, step - 1, way)
                ref[...] = (ref[...].astype(F32) + got[...].astype(F32)).astype(BF16)
            self.copy(k, step, way).start()
        if step > 1:
            self.drain(k, step - 1)

    def finish(self, k):
        last = self.half
        for way in range(2):
            self.copy(k, last, way).wait_recv()
        result = self.total[k, self.here].astype(F32)
        result = result + self.landing(k, last, 0)[...].astype(F32)
        result = result + self.landing(k, last, 1)[...].astype(F32)
        self.drain(k, last)
        return result


class Direct:
    def __init__(self, total, landing, size, here, device, send, recv, base):
        self.total, self.landing, self.size, self.here = total, landing, size, here
        self.device, self.send, self.recv, self.base = device, send, recv, base

    def copy(self, k, offset):
        place = lax.rem(self.here + offset, self.size)
        kind = self.base + offset - 1
        return pltpu.make_async_remote_copy(
            src_ref=self.total.at[k, place],
            dst_ref=self.landing.at[k, offset - 1],
            send_sem=self.send.at[lax.rem(k, SLOTS), kind],
            recv_sem=self.recv.at[k, kind],
            device_id=self.device(place),
            device_id_type=MESH,
        )

    def start(self, k):
        far_first = sorted(range(1, self.size), key=lambda o: -min(o, self.size - o))
        for offset in far_first:
            self.copy(k, offset).start()

    def drain(self, k):
        for offset in range(1, self.size):
            self.copy(k, offset).wait_send()

    def finish(self, k):
        for offset in range(1, self.size):
            self.copy(k, offset).wait_recv()
        result = self.total[k, self.here].astype(F32)
        for offset in range(1, self.size):
            result = result + self.landing[k, offset - 1].astype(F32)
        return result


def kernel(
    tok_in, table, cot_in, sv_hbm,
    act_out, tg_out, sg_out,
    agb, tok, tokt, sv, cot, part, rr, rl, hg,
    ta, ax1, ax2, ya, ay, tb, by1, by2, xb, bx,
    hgt, tgacc, tgs, tgr1, tgr2,
    sv_sem, tk_send, tk_recv, row_send, row_recv, ring_send, ring_recv, tg_send, tg_recv,
):
    dp, row, col = lax.axis_index("dp"), lax.axis_index("row"), lax.axis_index("col")
    x, y = lax.rem(dp, X), lax.div(dp, X)
    core, z = lax.rem(col, 2), lax.div(col, 2)
    x_right = (y * X + lax.rem(x + 1, X), row, col)
    x_left = (y * X + lax.rem(x + X - 1, X), row, col)
    y_right = (lax.rem(y + 1, Y) * X + x, row, col)
    y_left = (lax.rem(y + Y - 1, Y) * X + x, row, col)
    row_right, row_left = (dp, row + 1, col), (dp, row - 1, col)
    sibling = (dp, row, z * 2 + 1 - core)
    z_right, z_left = lax.rem(z + 1, Z), lax.rem(z + Z - 1, Z)
    dev_z_right, dev_z_left = (dp, row, z_right * 2 + core), (dp, row, z_left * 2 + core)

    load = pltpu.make_async_copy(sv_hbm, sv.at[pl.ds(0, CAP)], sv_sem)
    load.start()

    barrier = pltpu.get_barrier_semaphore()
    at_x = lambda place: (y * X + place, row, col)
    at_y = lambda place: (place * X + x, row, col)
    peers = [at_y(lax.rem(y + o, Y)) for o in range(1, Y)] + [at_x(lax.rem(x + o, X)) for o in range(1, X)]
    for other in [dev_z_right, dev_z_left] + peers + [sibling]:
        pl.semaphore_signal(barrier, inc=1, device_id=other, device_id_type=MESH)

    @pl.when(row < R - 1)
    def _():
        pl.semaphore_signal(barrier, inc=1, device_id=row_right, device_id_type=MESH)

    @pl.when(row > 0)
    def _():
        pl.semaphore_signal(barrier, inc=1, device_id=row_left, device_id_type=MESH)

    own = tok_in[...].astype(F32)
    for p in range(BT // 2):
        pair = [own[:, (2 * p + i) * BLK : (2 * p + i + 1) * BLK] for i in range(2)]
        agb[col, pl.ds(3 * p, 3)] = jnp.concatenate(pair, 0).astype(BF16).reshape(3, 16, BLK)

    pl.semaphore_wait(barrier, X + Y + 1 + (row < R - 1).astype(jnp.int32) + (row > 0).astype(jnp.int32))

    def token_copy(slot, piece, send, device):
        half = pl.ds(9 * piece, 9)
        return pltpu.make_async_remote_copy(
            src_ref=agb.at[slot, half],
            dst_ref=agb.at[slot, half],
            send_sem=tk_send.at[piece, send],
            recv_sem=tk_recv.at[piece, slot],
            device_id=device,
            device_id_type=MESH,
        )

    for piece in range(2):
        token_copy(col, piece, 0, dev_z_right).start()
        token_copy(col, piece, 1, dev_z_left).start()
        token_copy(col, piece, 2, sibling).start()

    last_rows = cot_in[pl.ds(32, 4), :].astype(F32)
    for k in range(NC):
        for jj in range(NJ):
            j = k * NJ + jj
            cot[k, pl.ds(2 * jj, 2)] = cot_in[pl.ds(0, 32), pl.ds(j * BLK, BLK)].reshape(2, 16, BLK)
        cot[k, 2 * NJ] = jnp.concatenate(
            [last_rows[:, (k * NJ + jj) * BLK : (k * NJ + jj + 1) * BLK] for jj in range(NJ)], 0
        ).astype(BF16)
    sv[CAP] = jnp.zeros((BLK, COLS * BLK), BF16)
    rr[:, 0] = jnp.zeros((NC, 2 * NJ + 1, 16, BLK), BF16)
    rl[:, R - 1] = jnp.zeros((NC, 2 * NJ + 1, 16, BLK), BF16)
    tgacc[...] = jnp.zeros(tgacc.shape, F32)
    tok[BT] = jnp.zeros((TOK, BLK), BF16)
    tokt[BT] = jnp.zeros((BLK, 2 * BLK), BF16)

    from_left, from_right = z_left * 2 + core, z_right * 2 + core
    def unpack(p, carry):
        pieces = [agb[c, pl.ds(3 * p, 3)].astype(F32).reshape(48, BLK) for c in range(2 * Z)]
        for i in range(2):
            full = jnp.concatenate([v[24 * i : 24 * i + 24] for v in pieces], 0)
            ordered = jnp.concatenate(
                [full[36 * r : 36 * r + 32] for r in range(R)]
                + [full[36 * r + 32 : 36 * r + 36] for r in range(R)]
                + [jnp.zeros((2 * BLK - TOK, BLK), F32)],
                0,
            )
            tok[2 * p + i] = ordered[:TOK].astype(BF16)
            tokt[2 * p + i] = ordered.T.astype(BF16)
        return carry

    for piece in range(2):
        token_copy(from_left, piece, 0, dev_z_right).wait_recv()
        token_copy(from_left, piece, 3, sibling).start()
        token_copy(from_right, piece, 0, dev_z_left).wait_recv()
        token_copy(from_right, piece, 4, sibling).start()
        for other in range(Z):
            token_copy(other * 2 + 1 - core, piece, 2, sibling).wait_recv()
        lax.fori_loop(3 * piece, 3 * piece + 3, unpack, 0)
    for piece in range(2):
        for send in range(5):
            token_copy(col, piece, send, sibling).wait_send()
    load.wait()

    ring_ax = Ring(ta, ax1, ax2, X, x, x_right, x_left, ring_send, ring_recv, 0)
    direct_ay = Direct(ya, ay, Y, y, at_y, ring_send, ring_recv, 4)
    ring_by = Ring(tb, by1, by2, Y, y, y_right, y_left, ring_send, ring_recv, 11)
    direct_bx = Direct(xb, bx, X, x, at_x, ring_send, ring_recv, 19)

    def by_path(k, x_first, y_first):
        y_path = functools.reduce(jnp.logical_or, [k == chunk for chunk in Y_CHUNKS])

        @pl.when(y_path)
        def _():
            y_first()

        @pl.when(jnp.logical_not(y_path))
        def _():
            x_first()

    def columns(j):
        return pl.ds(pl.multiple_of(j * BLK, BLK), BLK)

    def row_sum_copy(k, dest, way):
        return pltpu.make_async_remote_copy(
            src_ref=part.at[k, dest],
            dst_ref=(rl if way else rr).at[k, dest],
            send_sem=row_send.at[lax.rem(k, SLOTS), dest],
            recv_sem=row_recv.at[k, R * way + dest],
            device_id=row_left if way else row_right,
            device_id_type=MESH,
        )

    def row_sum_roles(step):
        return ((0, row == step - 1, range(R - 1, step - 1, -1)), (1, row == R - step, range(R - step)))

    def row_sum_drain(k, step):
        for way, mine, dests in row_sum_roles(step):

            @pl.when(mine)
            def _():
                for dest in dests:
                    row_sum_copy(k, dest, way).wait_send()

    def row_sum(k, step):
        for way, mine, dests in row_sum_roles(step):

            @pl.when(mine)
            def _():
                for dest in dests:
                    if step > 1:
                        row_sum_copy(k, dest, way).wait_recv()
                        got = (rl if way else rr)[k, dest].astype(F32)
                        part[k, dest] = (part[k, dest].astype(F32) + got).astype(BF16)
                    row_sum_copy(k, dest, way).start()

        if step > 1:
            row_sum_drain(k, step - 1)

    def gather_copy(k, source, step, way):
        return pltpu.make_async_remote_copy(
            src_ref=hg.at[k, source],
            dst_ref=hg.at[k, source],
            send_sem=row_send.at[lax.rem(k, SLOTS), R + 2 * step + way],
            recv_sem=row_recv.at[k, 2 * R + source],
            device_id=row_right if way == 0 else row_left,
            device_id_type=MESH,
        )

    def gather_sources(step):
        return (
            (0, row - step, (row >= step), row < R - 1),
            (1, row + step, (row + step < R), row > 0),
        )

    def gather_drain(k, step):
        for way, source, have, onward in gather_sources(step):

            @pl.when(have & onward)
            def _():
                gather_copy(k, source, step, way).wait_send()

    def gather(k, step):
        for way, source, have, onward in gather_sources(step):
            if step > 0:

                @pl.when(have)
                def _():
                    gather_copy(k, source, step - 1, way).wait_recv()

            if step < R - 1:

                @pl.when(have & onward)
                def _():
                    gather_copy(k, source, step, way).start()

        if step > 0:
            gather_drain(k, step - 1)

    def forward(k):
        ends = []
        for jj in range(NJ):
            j = k * NJ + jj
            picked = jnp.concatenate([tok[table[s, j]] for s in range(CAP)], 1)
            weight = sv[pl.ds(0, CAP), :, columns(j)].reshape(CAP * BLK, BLK)
            result = jnp.dot(picked, weight, preferred_element_type=F32)
            for d in range(R):
                part[k, d, pl.ds(2 * jj, 2)] = result[32 * d : 32 * d + 32].astype(BF16).reshape(2, 16, BLK)
            ends.append(result[32 * R :])
        for d in range(R):
            part[k, d, 2 * NJ] = jnp.concatenate([e[4 * d : 4 * d + 4] for e in ends], 0).astype(BF16)
        row_sum(k, 1)

    def activate(k):
        @pl.when(row > 0)
        def _():
            row_sum_copy(k, row, 0).wait_recv()

        @pl.when(row < R - 1)
        def _():
            row_sum_copy(k, row, 1).wait_recv()

        hidden = part[k, row].astype(F32) + rr[k, row].astype(F32) + rl[k, row].astype(F32)
        value, slope = gelu_pair(hidden)
        hg[k, row] = (cot[k].astype(F32) * slope).astype(BF16)
        gather(k, 0)
        act_out[k] = value.astype(BF16)
        row_sum_drain(k, R - 1)

    def grad_blocks(k):
        ends = [hg[k, s, 2 * NJ].astype(F32) for s in range(R)]
        blocks = []
        for jj in range(NJ):
            mains = [hg[k, s, pl.ds(2 * jj, 2)].reshape(32, BLK) for s in range(R)]
            end = jnp.concatenate([e[4 * jj : 4 * jj + 4] for e in ends], 0).astype(BF16)
            blocks.append(jnp.concatenate(mains + [end], 0))
        return blocks

    def weight_grad(k):
        blocks = grad_blocks(k)
        terms = []
        for jj in range(NJ):
            j = k * NJ + jj
            picked = jnp.concatenate([tokt[table[s, j]] for s in range(CAP)], 0)
            grad = jnp.concatenate([blocks[jj], jnp.zeros((2 * BLK - TOK, BLK), BF16)], 0)
            term = jnp.dot(picked, grad, preferred_element_type=F32)
            terms.append(term.astype(BF16).reshape(Y, X, 16, BLK))

        def x_first():
            for jj in range(NJ):
                for xx in range(X):
                    ta[k, xx, :, jj] = terms[jj][:, xx]
            ring_ax.advance(k, 1)

        def y_first():
            for jj in range(NJ):
                tb[k, :, :, jj] = terms[jj]
            ring_by.advance(k, 1)

        by_path(k, x_first, y_first)
        for jj in range(NJ):
            grad = jnp.concatenate([blocks[jj].astype(F32), jnp.zeros((2 * BLK - TOK, BLK), F32)], 0)
            hgt[pl.ds(jj * BLK, BLK), :] = grad.T.astype(BF16)

    def token_grad(k):
        grad = hgt[...]

        def pair(p, carry):
            weights = [
                jnp.concatenate(
                    [sv[table[CAP + 2 * p + i, k * NJ + jj], :, columns(k * NJ + jj)] for jj in range(NJ)],
                    1,
                )
                for i in range(2)
            ]
            tgacc[p] += jnp.dot(jnp.concatenate(weights, 0), grad, preferred_element_type=F32)
            return carry

        lax.fori_loop(0, BT // 2, pair, 0, unroll=True)

    def tg_copy(step):
        if step == 0:
            src, dst, device = tgs.at[1 - core], tgr1, sibling
        elif step == 1:
            src, dst, device = tgs.at[core, z_right], tgr2.at[0], dev_z_right
        else:
            src, dst, device = tgs.at[core, z_left], tgr2.at[1], dev_z_left
        return pltpu.make_async_remote_copy(
            src_ref=src,
            dst_ref=dst,
            send_sem=tg_send.at[step],
            recv_sem=tg_recv.at[step],
            device_id=device,
            device_id_type=MESH,
        )

    def tg_first():
        def pair(p, carry):
            both = tgacc[p].T
            pieces = []
            for i in range(2):
                v = both[:, i * BLK : (i + 1) * BLK]
                order = []
                for r in range(R):
                    order += [v[32 * r : 32 * r + 32], v[32 * R + 4 * r : 32 * R + 4 * r + 4]]
                pieces.append(jnp.concatenate(order, 0))
            for c in range(2 * Z):
                shard = jnp.concatenate([v[24 * c : 24 * c + 24] for v in pieces], 0)
                tgs[c % 2, c // 2, pl.ds(3 * p, 3)] = shard.astype(BF16).reshape(3, 16, BLK)
            return carry

        lax.fori_loop(0, BT // 2, pair, 0)
        tg_copy(0).start()

    def tg_second():
        tg_copy(0).wait_recv()
        tgs[core] = (tgs[core].astype(F32) + tgr1[...].astype(F32)).astype(BF16)
        tg_copy(1).start()
        tg_copy(2).start()
        tg_copy(0).wait_send()

    def tg_last():
        tg_copy(1).wait_recv()
        tg_copy(2).wait_recv()
        total = tgs[core, z].astype(F32) + tgr2[0].astype(F32) + tgr2[1].astype(F32)
        total = total.reshape(BT // 2, 48, BLK)
        for b in range(BT):
            tg_out[:, b * BLK : (b + 1) * BLK] = total[b // 2, 24 * (b % 2) : 24 * (b % 2) + 24].astype(BF16)
        tg_copy(1).wait_send()
        tg_copy(2).wait_send()

    factor = float(TOK * X * Y) ** (-0.5)

    def write(k, total):
        for jj in range(NJ):
            sg_out[:, columns(k * NJ + jj)] = total[jj] * factor

    def x_last(k):
        ya[k] = ring_ax.finish(k).astype(BF16)
        direct_ay.start(k)

    def x_first_sum(k):
        write(k, direct_ay.finish(k))
        direct_ay.drain(k)

    def y_last(k):
        xb[k] = ring_by.finish(k).astype(BF16)
        direct_bx.start(k)

    def y_first_sum(k):
        write(k, direct_bx.finish(k))
        direct_bx.drain(k)

    def only_x(work):
        return lambda k: by_path(k, lambda: work(k), lambda: None)

    def only_y(work):
        return lambda k: by_path(k, lambda: None, lambda: work(k))

    ready = 6 * LAG
    stages = (
        (0, forward),
        (LAG, lambda k: row_sum(k, 2)),
        (2 * LAG, lambda k: row_sum(k, 3)),
        (3 * LAG, activate),
        (4 * LAG, lambda k: gather(k, 1)),
        (5 * LAG, lambda k: gather(k, 2)),
        (ready + X_FIRST[0], only_x(lambda k: ring_ax.advance(k, 2))),
        (ready + Y_FIRST[2], only_y(lambda k: ring_by.advance(k, 4))),
        (ready + Y_FIRST[1], only_y(lambda k: ring_by.advance(k, 3))),
        (ready + Y_FIRST[0], only_y(lambda k: ring_by.advance(k, 2))),
        (ready + X_FIRST[1], only_x(x_last)),
        (ready + Y_FIRST[3], only_y(y_last)),
        (ready, lambda k: gather(k, 3)),
        (ready, weight_grad),
        (ready, token_grad),
        (ready + X_FIRST[2], only_x(x_first_sum)),
        (ready + Y_FIRST[4], only_y(y_first_sum)),
    )

    def tick(t, carry):
        for stage, work in stages:
            k = t - stage

            @pl.when((k >= 0) & (k < NC))
            def _():
                work(k)

        for stage, work in ((ready, tg_first), (ready + X_FIRST[0], tg_second)):

            @pl.when(t == NC - 1 + stage)
            def _():
                work()

        return carry

    ticks = max(NC + ready + X_FIRST[2], Y_CHUNKS[-1] + 1 + ready + Y_FIRST[4])
    lax.fori_loop(0, ticks, tick, 0)
    tg_last()


def body(tokens_in, slot_values, slot_rows, act_cotangent):
    blocks = jnp.arange(BT, dtype=jnp.int32)
    slots = jnp.arange(CAP, dtype=jnp.int32)
    match = slot_rows[None, :, :] == blocks[:, None, None]
    inverse = jnp.min(jnp.where(match, slots[None, :, None], CAP), axis=1)
    table = jnp.concatenate([slot_rows, inverse], axis=0)

    def dma(*shape):
        return pltpu.SemaphoreType.DMA(shape)

    def buf(*shape, dtype=BF16):
        return pltpu.VMEM(shape, dtype)

    vmem = pl.BlockSpec(memory_space=pltpu.VMEM)
    smem = pl.BlockSpec(memory_space=pltpu.SMEM)
    tiles = 2 * NJ + 1
    packed, token_grad, summed = pl.pallas_call(
        kernel,
        out_shape=(
            jax.ShapeDtypeStruct((NC, tiles, 16, BLK), BF16),
            jax.ShapeDtypeStruct((24, BT * BLK), BF16),
            jax.ShapeDtypeStruct((16, COLS * BLK), F32),
        ),
        in_specs=[vmem, smem, vmem, pl.BlockSpec(memory_space=pl.ANY)],
        out_specs=(vmem, vmem, vmem),
        scratch_shapes=[
            buf(2 * Z, 18, 16, BLK),
            buf(BT + 1, TOK, BLK),
            buf(BT + 1, BLK, 2 * BLK),
            buf(CAP + 1, BLK, COLS * BLK),
            buf(NC, tiles, 16, BLK),
            buf(NC, R, tiles, 16, BLK),
            buf(NC, R, tiles, 16, BLK),
            buf(NC, R, tiles, 16, BLK),
            buf(NC, R, tiles, 16, BLK),
            buf(NC, X, Y, NJ, 16, BLK),
            buf(NC, 2, Y // 2, NJ, 16, BLK),
            buf(NC, 1, 2, Y, NJ, 16, BLK),
            buf(NC, Y, NJ, 16, BLK),
            buf(NC, Y - 1, NJ, 16, BLK),
            buf(NC, Y, X, NJ, 16, BLK),
            buf(NC, 2, X // 2, NJ, 16, BLK),
            buf(NC, 3, 2, X, NJ, 16, BLK),
            buf(NC, X, NJ, 16, BLK),
            buf(NC, X - 1, NJ, 16, BLK),
            buf(NJ * BLK, 2 * BLK),
            buf(BT // 2, 2 * BLK, 2 * BLK, dtype=F32),
            buf(2, Z, 18, 16, BLK),
            buf(Z, 18, 16, BLK),
            buf(2, 18, 16, BLK),
            pltpu.SemaphoreType.DMA,
            dma(2, 5),
            dma(2, 2 * Z),
            dma(SLOTS, R + 6),
            dma(NC, 3 * R),
            dma(SLOTS, 22),
            dma(NC, 22),
            dma(3),
            dma(3),
        ],
        compiler_params=pltpu.CompilerParams(
            collective_id=0, has_side_effects=True, vmem_limit_bytes=52 * 1024 * 1024
        ),
    )(tokens_in, table, act_cotangent, slot_values.reshape(CAP, BLK, COLS * BLK))

    mains = packed[:, : 2 * NJ].reshape(NC, NJ, 32, BLK)
    ends = packed[:, 2 * NJ].reshape(NC, NJ, 4, BLK)
    activation = jnp.concatenate([mains, ends], axis=2).transpose(2, 0, 1, 3).reshape(36, COLS * BLK)
    slot_grad = summed.reshape(16, 1, COLS * BLK)
    return (activation, token_grad, slot_grad)


def solution(mesh):
    return jax.shard_map(
        body,
        mesh=mesh,
        in_specs=(
            P(("dp", "col"), "row"),
            P("row", "col"),
            P("row", "col"),
            P(("dp", "row"), "col"),
        ),
        out_specs=(P(("dp", "row"), "col"), P(("dp", "col"), "row"), P("dp", "row", "col")),
        check_vma=False,
    )
```

```python
import functools

import jax
import jax.numpy as jnp
from jax import lax
from jax.experimental import pallas as pl
from jax.experimental.pallas import tpu as pltpu
from jax.sharding import PartitionSpec as P

MESH = pl.DeviceIdType.MESH
BF16 = jnp.bfloat16
F32 = jnp.float32

BLK = 128
CAP = 4
BT = 12
COLS = 32
X, Y = 4, 8
R = 4
Z = 3
TOK = 144
NC = 8
NJ = COLS // NC
LAG = 1
X_FIRST = (2, 4, 7)
Y_FIRST = (2, 4, 6, 8, 11)
Y_CHUNKS = (0, 3)
SLOTS = 4

root_two_pi = 0.7978845608028654
cubic_coef = 0.044715


def gelu_pair(hidden):
    inner = root_two_pi * (hidden + cubic_coef * hidden * hidden * hidden)
    tangent = jnp.tanh(inner)
    value = 0.5 * hidden * (1.0 + tangent)
    slope = 0.5 * (1.0 + tangent) + 0.5 * hidden * (1.0 - tangent * tangent) * root_two_pi * (
        1.0 + 3.0 * cubic_coef * hidden * hidden
    )
    return (value, slope)


class Ring:
    def __init__(self, total, first, later, size, here, right, left, send, recv, base):
        self.total, self.first, self.later = total, first, later
        self.size, self.here, self.right, self.left = size, here, right, left
        self.send, self.recv, self.base = send, recv, base
        self.half = size // 2

    def shard(self, k, step, way):
        offset = self.half + 1 - step
        place = lax.rem(self.here + (offset if way == 0 else self.size - offset), self.size)
        ref = self.total.at[k, place]
        if step == 1:
            part = self.total.shape[2] // 2
            return ref.at[pl.ds(way * part, part)]
        return ref

    def landing(self, k, step, way):
        return self.first.at[k, way] if step == 1 else self.later.at[k, step - 2, way]

    def copy(self, k, step, way):
        kind = self.base + 2 * (step - 1) + way
        return pltpu.make_async_remote_copy(
            src_ref=self.shard(k, step, way),
            dst_ref=self.landing(k, step, way),
            send_sem=self.send.at[lax.rem(k, SLOTS), kind],
            recv_sem=self.recv.at[k, kind],
            device_id=self.right if way == 0 else self.left,
            device_id_type=MESH,
        )

    def drain(self, k, step):
        for way in range(2):
            self.copy(k, step, way).wait_send()

    def advance(self, k, step):
        for way in range(2):
            if step > 1:
                self.copy(k, step - 1, way).wait_recv()
                ref = self.shard(k, step, way)
                if step == 2:
                    part = self.total.shape[2] // 2
                    ref = ref.at[pl.ds(way * part, part)]
                got = self.landing(k, step - 1, way)
                ref[...] = (ref[...].astype(F32) + got[...].astype(F32)).astype(BF16)
            self.copy(k, step, way).start()
        if step > 1:
            self.drain(k, step - 1)

    def finish(self, k):
        last = self.half
        for way in range(2):
            self.copy(k, last, way).wait_recv()
        result = self.total[k, self.here].astype(F32)
        result = result + self.landing(k, last, 0)[...].astype(F32)
        result = result + self.landing(k, last, 1)[...].astype(F32)
        self.drain(k, last)
        return result


class Direct:
    def __init__(self, total, landing, size, here, device, send, recv, base):
        self.total, self.landing, self.size, self.here = total, landing, size, here
        self.device, self.send, self.recv, self.base = device, send, recv, base

    def copy(self, k, offset):
        place = lax.rem(self.here + offset, self.size)
        kind = self.base + offset - 1
        return pltpu.make_async_remote_copy(
            src_ref=self.total.at[k, place],
            dst_ref=self.landing.at[k, offset - 1],
            send_sem=self.send.at[lax.rem(k, SLOTS), kind],
            recv_sem=self.recv.at[k, kind],
            device_id=self.device(place),
            device_id_type=MESH,
        )

    def start(self, k):
        far_first = sorted(range(1, self.size), key=lambda o: -min(o, self.size - o))
        for offset in far_first:
            self.copy(k, offset).start()

    def drain(self, k):
        for offset in range(1, self.size):
            self.copy(k, offset).wait_send()

    def finish(self, k):
        for offset in range(1, self.size):
            self.copy(k, offset).wait_recv()
        result = self.total[k, self.here].astype(F32)
        for offset in range(1, self.size):
            result = result + self.landing[k, offset - 1].astype(F32)
        return result


def kernel(
    tok_in, table, cot_in, sv_hbm,
    act_out, tg_out, sg_out,
    agb, tok, tokt, sv, cot, part, rr, rl, hg,
    ta, ax1, ax2, ya, ay, tb, by1, by2, xb, bx,
    hgt, tgacc, tgs, tgr1, tgr2,
    sv_sem, tk_send, tk_recv, row_send, row_recv, ring_send, ring_recv, tg_send, tg_recv,
):
    dp, row, col = lax.axis_index("dp"), lax.axis_index("row"), lax.axis_index("col")
    x, y = lax.rem(dp, X), lax.div(dp, X)
    core, z = lax.rem(col, 2), lax.div(col, 2)
    x_right = (y * X + lax.rem(x + 1, X), row, col)
    x_left = (y * X + lax.rem(x + X - 1, X), row, col)
    y_right = (lax.rem(y + 1, Y) * X + x, row, col)
    y_left = (lax.rem(y + Y - 1, Y) * X + x, row, col)
    row_right, row_left = (dp, row + 1, col), (dp, row - 1, col)
    sibling = (dp, row, z * 2 + 1 - core)
    z_right, z_left = lax.rem(z + 1, Z), lax.rem(z + Z - 1, Z)
    dev_z_right, dev_z_left = (dp, row, z_right * 2 + core), (dp, row, z_left * 2 + core)

    load = pltpu.make_async_copy(sv_hbm, sv.at[pl.ds(0, CAP)], sv_sem)
    load.start()

    barrier = pltpu.get_barrier_semaphore()
    at_x = lambda place: (y * X + place, row, col)
    at_y = lambda place: (place * X + x, row, col)
    peers = [at_y(lax.rem(y + o, Y)) for o in range(1, Y)] + [at_x(lax.rem(x + o, X)) for o in range(1, X)]
    for other in [dev_z_right, dev_z_left] + peers + [sibling]:
        pl.semaphore_signal(barrier, inc=1, device_id=other, device_id_type=MESH)

    @pl.when(row < R - 1)
    def _():
        pl.semaphore_signal(barrier, inc=1, device_id=row_right, device_id_type=MESH)

    @pl.when(row > 0)
    def _():
        pl.semaphore_signal(barrier, inc=1, device_id=row_left, device_id_type=MESH)

    own = tok_in[...].astype(F32)
    for p in range(BT // 2):
        pair = [own[:, (2 * p + i) * BLK : (2 * p + i + 1) * BLK] for i in range(2)]
        agb[col, pl.ds(3 * p, 3)] = jnp.concatenate(pair, 0).astype(BF16).reshape(3, 16, BLK)

    pl.semaphore_wait(barrier, X + Y + 1 + (row < R - 1).astype(jnp.int32) + (row > 0).astype(jnp.int32))

    def token_copy(slot, piece, send, device):
        half = pl.ds(9 * piece, 9)
        return pltpu.make_async_remote_copy(
            src_ref=agb.at[slot, half],
            dst_ref=agb.at[slot, half],
            send_sem=tk_send.at[piece, send],
            recv_sem=tk_recv.at[piece, slot],
            device_id=device,
            device_id_type=MESH,
        )

    for piece in range(2):
        token_copy(col, piece, 0, dev_z_right).start()
        token_copy(col, piece, 1, dev_z_left).start()
        token_copy(col, piece, 2, sibling).start()

    last_rows = cot_in[pl.ds(32, 4), :].astype(F32)
    for k in range(NC):
        for jj in range(NJ):
            j = k * NJ + jj
            cot[k, pl.ds(2 * jj, 2)] = cot_in[pl.ds(0, 32), pl.ds(j * BLK, BLK)].reshape(2, 16, BLK)
        cot[k, 2 * NJ] = jnp.concatenate(
            [last_rows[:, (k * NJ + jj) * BLK : (k * NJ + jj + 1) * BLK] for jj in range(NJ)], 0
        ).astype(BF16)
    sv[CAP] = jnp.zeros((BLK, COLS * BLK), BF16)
    rr[:, 0] = jnp.zeros((NC, 2 * NJ + 1, 16, BLK), BF16)
    rl[:, R - 1] = jnp.zeros((NC, 2 * NJ + 1, 16, BLK), BF16)
    tgacc[...] = jnp.zeros(tgacc.shape, F32)
    tok[BT] = jnp.zeros((TOK, BLK), BF16)
    tokt[BT] = jnp.zeros((BLK, 2 * BLK), BF16)

    from_left, from_right = z_left * 2 + core, z_right * 2 + core
    def unpack(p, carry):
        pieces = [agb[c, pl.ds(3 * p, 3)].astype(F32).reshape(48, BLK) for c in range(2 * Z)]
        for i in range(2):
            full = jnp.concatenate([v[24 * i : 24 * i + 24] for v in pieces], 0)
            ordered = jnp.concatenate(
                [full[36 * r : 36 * r + 32] for r in range(R)]
                + [full[36 * r + 32 : 36 * r + 36] for r in range(R)]
                + [jnp.zeros((2 * BLK - TOK, BLK), F32)],
                0,
            )
            tok[2 * p + i] = ordered[:TOK].astype(BF16)
            tokt[2 * p + i] = ordered.T.astype(BF16)
        return carry

    for piece in range(2):
        token_copy(from_left, piece, 0, dev_z_right).wait_recv()
        token_copy(from_left, piece, 3, sibling).start()
        token_copy(from_right, piece, 0, dev_z_left).wait_recv()
        token_copy(from_right, piece, 4, sibling).start()
        for other in range(Z):
            token_copy(other * 2 + 1 - core, piece, 2, sibling).wait_recv()
        lax.fori_loop(3 * piece, 3 * piece + 3, unpack, 0)
    for piece in range(2):
        for send in range(5):
            token_copy(col, piece, send, sibling).wait_send()
    load.wait()

    ring_ax = Ring(ta, ax1, ax2, X, x, x_right, x_left, ring_send, ring_recv, 0)
    direct_ay = Direct(ya, ay, Y, y, at_y, ring_send, ring_recv, 4)
    ring_by = Ring(tb, by1, by2, Y, y, y_right, y_left, ring_send, ring_recv, 11)
    direct_bx = Direct(xb, bx, X, x, at_x, ring_send, ring_recv, 19)

    def by_path(k, x_first, y_first):
        y_path = functools.reduce(jnp.logical_or, [k == chunk for chunk in Y_CHUNKS])

        @pl.when(y_path)
        def _():
            y_first()

        @pl.when(jnp.logical_not(y_path))
        def _():
            x_first()

    def columns(j):
        return pl.ds(pl.multiple_of(j * BLK, BLK), BLK)

    def row_sum_copy(k, dest, way):
        return pltpu.make_async_remote_copy(
            src_ref=part.at[k, dest],
            dst_ref=(rl if way else rr).at[k, dest],
            send_sem=row_send.at[lax.rem(k, SLOTS), dest],
            recv_sem=row_recv.at[k, R * way + dest],
            device_id=row_left if way else row_right,
            device_id_type=MESH,
        )

    def row_sum_roles(step):
        return ((0, row == step - 1, range(R - 1, step - 1, -1)), (1, row == R - step, range(R - step)))

    def row_sum_drain(k, step):
        for way, mine, dests in row_sum_roles(step):

            @pl.when(mine)
            def _():
                for dest in dests:
                    row_sum_copy(k, dest, way).wait_send()

    def row_sum(k, step):
        for way, mine, dests in row_sum_roles(step):

            @pl.when(mine)
            def _():
                for dest in dests:
                    if step > 1:
                        row_sum_copy(k, dest, way).wait_recv()
                        got = (rl if way else rr)[k, dest].astype(F32)
                        part[k, dest] = (part[k, dest].astype(F32) + got).astype(BF16)
                    row_sum_copy(k, dest, way).start()

        if step > 1:
            row_sum_drain(k, step - 1)

    def gather_copy(k, source, step, way):
        return pltpu.make_async_remote_copy(
            src_ref=hg.at[k, source],
            dst_ref=hg.at[k, source],
            send_sem=row_send.at[lax.rem(k, SLOTS), R + 2 * step + way],
            recv_sem=row_recv.at[k, 2 * R + source],
            device_id=row_right if way == 0 else row_left,
            device_id_type=MESH,
        )

    def gather_sources(step):
        return (
            (0, row - step, (row >= step), row < R - 1),
            (1, row + step, (row + step < R), row > 0),
        )

    def gather_drain(k, step):
        for way, source, have, onward in gather_sources(step):

            @pl.when(have & onward)
            def _():
                gather_copy(k, source, step, way).wait_send()

    def gather(k, step):
        for way, source, have, onward in gather_sources(step):
            if step > 0:

                @pl.when(have)
                def _():
                    gather_copy(k, source, step - 1, way).wait_recv()

            if step < R - 1:

                @pl.when(have & onward)
                def _():
                    gather_copy(k, source, step, way).start()

        if step > 0:
            gather_drain(k, step - 1)

    def forward(k):
        ends = []
        for jj in range(NJ):
            j = k * NJ + jj
            picked = jnp.concatenate([tok[table[s, j]] for s in range(CAP)], 1)
            weight = sv[pl.ds(0, CAP), :, columns(j)].reshape(CAP * BLK, BLK)
            result = jnp.dot(picked, weight, preferred_element_type=F32)
            for d in range(R):
                part[k, d, pl.ds(2 * jj, 2)] = result[32 * d : 32 * d + 32].astype(BF16).reshape(2, 16, BLK)
            ends.append(result[32 * R :])
        for d in range(R):
            part[k, d, 2 * NJ] = jnp.concatenate([e[4 * d : 4 * d + 4] for e in ends], 0).astype(BF16)
        row_sum(k, 1)

    def activate(k):
        @pl.when(row > 0)
        def _():
            row_sum_copy(k, row, 0).wait_recv()

        @pl.when(row < R - 1)
        def _():
            row_sum_copy(k, row, 1).wait_recv()

        hidden = part[k, row].astype(F32) + rr[k, row].astype(F32) + rl[k, row].astype(F32)
        value, slope = gelu_pair(hidden)
        hg[k, row] = (cot[k].astype(F32) * slope).astype(BF16)
        gather(k, 0)
        for jj in range(NJ):
            act_out[pl.ds(0, 32), columns(k * NJ + jj)] = value[2 * jj : 2 * jj + 2].reshape(32, BLK).astype(BF16)
            act_out[pl.ds(32, 4), columns(k * NJ + jj)] = value[2 * NJ, 4 * jj : 4 * jj + 4].astype(BF16)
        row_sum_drain(k, R - 1)

    def grad_blocks(k):
        ends = [hg[k, s, 2 * NJ].astype(F32) for s in range(R)]
        blocks = []
        for jj in range(NJ):
            mains = [hg[k, s, pl.ds(2 * jj, 2)].reshape(32, BLK) for s in range(R)]
            end = jnp.concatenate([e[4 * jj : 4 * jj + 4] for e in ends], 0).astype(BF16)
            blocks.append(jnp.concatenate(mains + [end], 0))
        return blocks

    def weight_grad(k):
        blocks = grad_blocks(k)
        terms = []
        for jj in range(NJ):
            j = k * NJ + jj
            picked = jnp.concatenate([tokt[table[s, j]] for s in range(CAP)], 0)
            grad = jnp.concatenate([blocks[jj], jnp.zeros((2 * BLK - TOK, BLK), BF16)], 0)
            term = jnp.dot(picked, grad, preferred_element_type=F32)
            terms.append(term.astype(BF16).reshape(Y, X, 16, BLK))

        def x_first():
            for jj in range(NJ):
                for xx in range(X):
                    ta[k, xx, :, jj] = terms[jj][:, xx]
            ring_ax.advance(k, 1)

        def y_first():
            for jj in range(NJ):
                tb[k, :, :, jj] = terms[jj]
            ring_by.advance(k, 1)

        by_path(k, x_first, y_first)
        for jj in range(NJ):
            grad = jnp.concatenate([blocks[jj].astype(F32), jnp.zeros((2 * BLK - TOK, BLK), F32)], 0)
            hgt[pl.ds(jj * BLK, BLK), :] = grad.T.astype(BF16)

    def token_grad(k):
        grad = hgt[...]

        def pair(p, carry):
            weights = [
                jnp.concatenate(
                    [sv[table[CAP + 2 * p + i, k * NJ + jj], :, columns(k * NJ + jj)] for jj in range(NJ)],
                    1,
                )
                for i in range(2)
            ]
            tgacc[p] += jnp.dot(jnp.concatenate(weights, 0), grad, preferred_element_type=F32)
            return carry

        lax.fori_loop(0, BT // 2, pair, 0, unroll=True)

    def tg_copy(step):
        if step == 0:
            src, dst, device = tgs.at[1 - core], tgr1, sibling
        elif step == 1:
            src, dst, device = tgs.at[core, z_right], tgr2.at[0], dev_z_right
        else:
            src, dst, device = tgs.at[core, z_left], tgr2.at[1], dev_z_left
        return pltpu.make_async_remote_copy(
            src_ref=src,
            dst_ref=dst,
            send_sem=tg_send.at[step],
            recv_sem=tg_recv.at[step],
            device_id=device,
            device_id_type=MESH,
        )

    def tg_first():
        def pair(p, carry):
            both = tgacc[p].T
            pieces = []
            for i in range(2):
                v = both[:, i * BLK : (i + 1) * BLK]
                order = []
                for r in range(R):
                    order += [v[32 * r : 32 * r + 32], v[32 * R + 4 * r : 32 * R + 4 * r + 4]]
                pieces.append(jnp.concatenate(order, 0))
            for c in range(2 * Z):
                shard = jnp.concatenate([v[24 * c : 24 * c + 24] for v in pieces], 0)
                tgs[c % 2, c // 2, pl.ds(3 * p, 3)] = shard.astype(BF16).reshape(3, 16, BLK)
            return carry

        lax.fori_loop(0, BT // 2, pair, 0)
        tg_copy(0).start()

    def tg_second():
        tg_copy(0).wait_recv()
        tgs[core] = (tgs[core].astype(F32) + tgr1[...].astype(F32)).astype(BF16)
        tg_copy(1).start()
        tg_copy(2).start()
        tg_copy(0).wait_send()

    def tg_last():
        tg_copy(1).wait_recv()
        tg_copy(2).wait_recv()
        total = tgs[core, z].astype(F32) + tgr2[0].astype(F32) + tgr2[1].astype(F32)
        total = total.reshape(BT // 2, 48, BLK)
        for b in range(BT):
            tg_out[:, b * BLK : (b + 1) * BLK] = total[b // 2, 24 * (b % 2) : 24 * (b % 2) + 24].astype(BF16)
        tg_copy(1).wait_send()
        tg_copy(2).wait_send()

    factor = float(TOK * X * Y) ** (-0.5)

    def write(k, total):
        for jj in range(NJ):
            sg_out[:, columns(k * NJ + jj)] = total[jj] * factor

    def x_last(k):
        ya[k] = ring_ax.finish(k).astype(BF16)
        direct_ay.start(k)

    def x_first_sum(k):
        write(k, direct_ay.finish(k))
        direct_ay.drain(k)

    def y_last(k):
        xb[k] = ring_by.finish(k).astype(BF16)
        direct_bx.start(k)

    def y_first_sum(k):
        write(k, direct_bx.finish(k))
        direct_bx.drain(k)

    def only_x(work):
        return lambda k: by_path(k, lambda: work(k), lambda: None)

    def only_y(work):
        return lambda k: by_path(k, lambda: None, lambda: work(k))

    ready = 6 * LAG
    stages = (
        (0, forward),
        (LAG, lambda k: row_sum(k, 2)),
        (2 * LAG, lambda k: row_sum(k, 3)),
        (3 * LAG, activate),
        (4 * LAG, lambda k: gather(k, 1)),
        (5 * LAG, lambda k: gather(k, 2)),
        (ready + X_FIRST[0], only_x(lambda k: ring_ax.advance(k, 2))),
        (ready + Y_FIRST[2], only_y(lambda k: ring_by.advance(k, 4))),
        (ready + Y_FIRST[1], only_y(lambda k: ring_by.advance(k, 3))),
        (ready + Y_FIRST[0], only_y(lambda k: ring_by.advance(k, 2))),
        (ready + X_FIRST[1], only_x(x_last)),
        (ready + Y_FIRST[3], only_y(y_last)),
        (ready, lambda k: gather(k, 3)),
        (ready, weight_grad),
        (ready, token_grad),
        (ready + X_FIRST[2], only_x(x_first_sum)),
        (ready + Y_FIRST[4], only_y(y_first_sum)),
    )

    def tick(t, carry):
        for stage, work in stages:
            k = t - stage

            @pl.when((k >= 0) & (k < NC))
            def _():
                work(k)

        for stage, work in ((ready, tg_first), (ready + X_FIRST[0], tg_second)):

            @pl.when(t == NC - 1 + stage)
            def _():
                work()

        return carry

    ticks = max(NC + ready + X_FIRST[2], Y_CHUNKS[-1] + 1 + ready + Y_FIRST[4])
    lax.fori_loop(0, ticks, tick, 0)
    tg_last()


def body(tokens_in, slot_values, slot_rows, act_cotangent):
    blocks = jnp.arange(BT, dtype=jnp.int32)
    slots = jnp.arange(CAP, dtype=jnp.int32)
    match = slot_rows[None, :, :] == blocks[:, None, None]
    inverse = jnp.min(jnp.where(match, slots[None, :, None], CAP), axis=1)
    table = jnp.concatenate([slot_rows, inverse], axis=0)

    def dma(*shape):
        return pltpu.SemaphoreType.DMA(shape)

    def buf(*shape, dtype=BF16):
        return pltpu.VMEM(shape, dtype)

    vmem = pl.BlockSpec(memory_space=pltpu.VMEM)
    smem = pl.BlockSpec(memory_space=pltpu.SMEM)
    tiles = 2 * NJ + 1
    activation, token_grad, summed = pl.pallas_call(
        kernel,
        out_shape=(
            jax.ShapeDtypeStruct((36, COLS * BLK), BF16),
            jax.ShapeDtypeStruct((24, BT * BLK), BF16),
            jax.ShapeDtypeStruct((16, COLS * BLK), F32),
        ),
        in_specs=[vmem, smem, vmem, pl.BlockSpec(memory_space=pl.ANY)],
        out_specs=(vmem, vmem, vmem),
        scratch_shapes=[
            buf(2 * Z, 18, 16, BLK),
            buf(BT + 1, TOK, BLK),
            buf(BT + 1, BLK, 2 * BLK),
            buf(CAP + 1, BLK, COLS * BLK),
            buf(NC, tiles, 16, BLK),
            buf(NC, R, tiles, 16, BLK),
            buf(NC, R, tiles, 16, BLK),
            buf(NC, R, tiles, 16, BLK),
            buf(NC, R, tiles, 16, BLK),
            buf(NC, X, Y, NJ, 16, BLK),
            buf(NC, 2, Y // 2, NJ, 16, BLK),
            buf(NC, 1, 2, Y, NJ, 16, BLK),
            buf(NC, Y, NJ, 16, BLK),
            buf(NC, Y - 1, NJ, 16, BLK),
            buf(NC, Y, X, NJ, 16, BLK),
            buf(NC, 2, X // 2, NJ, 16, BLK),
            buf(NC, 3, 2, X, NJ, 16, BLK),
            buf(NC, X, NJ, 16, BLK),
            buf(NC, X - 1, NJ, 16, BLK),
            buf(NJ * BLK, 2 * BLK),
            buf(BT // 2, 2 * BLK, 2 * BLK, dtype=F32),
            buf(2, Z, 18, 16, BLK),
            buf(Z, 18, 16, BLK),
            buf(2, 18, 16, BLK),
            pltpu.SemaphoreType.DMA,
            dma(2, 5),
            dma(2, 2 * Z),
            dma(SLOTS, R + 6),
            dma(NC, 3 * R),
            dma(SLOTS, 22),
            dma(NC, 22),
            dma(3),
            dma(3),
        ],
        compiler_params=pltpu.CompilerParams(
            collective_id=0, has_side_effects=True, vmem_limit_bytes=52 * 1024 * 1024
        ),
    )(tokens_in, table, act_cotangent, slot_values.reshape(CAP, BLK, COLS * BLK))

    slot_grad = summed.reshape(16, 1, COLS * BLK)
    return (activation, token_grad, slot_grad)


def solution(mesh):
    return jax.shard_map(
        body,
        mesh=mesh,
        in_specs=(
            P(("dp", "col"), "row"),
            P("row", "col"),
            P("row", "col"),
            P(("dp", "row"), "col"),
        ),
        out_specs=(P(("dp", "row"), "col"), P(("dp", "col"), "row"), P("dp", "row", "col")),
        check_vma=False,
    )
```
